256 devices in a mesh: sec: 16 (over x, z_hi, core), tile: 16 (over y, z_lo).
Axes of the slice: x: 4, y: 4, z: 8 (z_hi: 2, z_lo: 4; z = z_hi * 4 + z_lo), core: 2. Of those that a mesh axis runs over, the one named last changes fastest.
Arguments:
- sections: float32 [16, 16, 256, 512], P('sec', 'tile'), may hold values from -41 to 41
- following: float32 [16, 448, 704], P('tile'), may hold values from -41 to 41, as said below
Outputs:
- flow: float32 [16, 16, 2, 32], P('sec', 'tile')
- strength: float32 [16, 16, 32], P('sec', 'tile')
The draws below stay inside these ranges and needn't reach their ends.
Inputs may be any that keep to these rules, and one draw needn't show every extreme that they name: `following`: tile t = 4 * r + c holds the 448 by 512 + 3 * 64 cells of that section from row 256 * r - 96 and column 512 * c - 96, with 0 outside the section.
All inputs are finite; a program needn't handle non-finite values.
Results may differ from the reference program's by a relative error of at most 0.029.
Values sent between devices are 32-bit elements; how exact they have to be, the bound alone decides.
A program may use at most 64 MiB of HBM per device.

```python
import math
import jax
import jax.numpy as jnp
from jax import lax

PATCH = 128
TCOLS = 4
TH = 256
TW = 512
NSEC = 16
TILES = 16


def stack_draw(key, contrast):
    grid_rows = TILES // TCOLS
    height = grid_rows * TH
    breadth = TCOLS * TW
    reach_cells = PATCH // 4 - 1
    border = 2 * reach_cells
    cell_size = max(PATCH // 16, 2)
    pieces = jax.random.split(key, 9)
    tall_size = height + 2 * border
    broad_size = breadth + 2 * border
    coarse = jax.random.normal(pieces[0], (tall_size // cell_size + 2, broad_size // cell_size + 2), jnp.float32)
    row_index = jnp.arange(tall_size, dtype=jnp.int32)
    col_index = jnp.arange(broad_size, dtype=jnp.int32)
    row_cell = (row_index // cell_size)[:, None]
    col_cell = (col_index // cell_size)[None, :]
    row_frac = ((row_index % cell_size).astype(jnp.float32) / cell_size)[:, None]
    col_frac = ((col_index % cell_size).astype(jnp.float32) / cell_size)[None, :]
    corner_aa = coarse[row_cell, col_cell]
    corner_ab = coarse[row_cell, col_cell + 1]
    corner_ba = coarse[row_cell + 1, col_cell]
    corner_bb = coarse[row_cell + 1, col_cell + 1]
    smooth = (1.0 - row_frac) * (1.0 - col_frac) * corner_aa + (1.0 - row_frac) * col_frac * corner_ab + row_frac * (1.0 - col_frac) * corner_ba + row_frac * col_frac * corner_bb
    rough_part = jax.random.normal(pieces[1], (tall_size, broad_size), jnp.float32)
    ground = 1.2 * smooth + 0.6 * rough_part
    section_count = NSEC + 1
    blocks_down = height // PATCH
    blocks_across = breadth // PATCH
    shift_shape = (section_count, 2, blocks_down, blocks_across)
    magnitude = jnp.maximum(jax.random.randint(pieces[2], shift_shape, 0, reach_cells + 1), jax.random.randint(pieces[7], shift_shape, 0, reach_cells + 1))
    direction_sign = 2 * jax.random.randint(pieces[8], shift_shape, 0, 2) - 1
    displace = direction_sign * magnitude
    flawed = jax.random.randint(pieces[3], (section_count, blocks_down, blocks_across), 0, 8)
    down_block = jnp.arange(height, dtype=jnp.int32) // PATCH
    across_block = jnp.arange(breadth, dtype=jnp.int32) // PATCH
    shift_down = displace[:, 0][:, down_block][:, :, across_block]
    shift_across = displace[:, 1][:, down_block][:, :, across_block]
    source_row = jnp.arange(height, dtype=jnp.int32)[None, :, None] + border - shift_down
    source_col = jnp.arange(breadth, dtype=jnp.int32)[None, None, :] + border - shift_across
    displaced = ground[source_row, source_col]
    foreign = 1.3 * jax.random.normal(pieces[4], (section_count, height, breadth), jnp.float32)
    broken = flawed[:, down_block][:, :, across_block] == 0
    noise = 0.3 * jax.random.normal(pieces[5], (section_count, height, breadth), jnp.float32)
    imagery = jnp.clip(jnp.where(broken, foreign, displaced) + noise, -4.0, 4.0)
    stride = PATCH // 2
    contrast_level = jax.random.uniform(pieces[6], (height // stride, breadth // stride), jnp.float32)
    gain_field = 10.0 ** (contrast * contrast_level)
    gain_cells = gain_field[(jnp.arange(height, dtype=jnp.int32) // stride)[:, None], (jnp.arange(breadth, dtype=jnp.int32) // stride)[None, :]]
    return imagery * gain_cells[None]


def into_tiles(imagery):
    section_count = imagery.shape[0]
    grid_rows = TILES // TCOLS
    return imagery.reshape(section_count, grid_rows, TH, TCOLS, TW).transpose(0, 1, 3, 2, 4).reshape(section_count, TILES, TH, TW)


def draw_sections(key, part):
    imagery = stack_draw(key, 0.0)
    return into_tiles(imagery[:NSEC])


def draw_following(key, part):
    imagery = stack_draw(key, 0.0)
    margin = 3 * PATCH // 4
    padded = jnp.pad(imagery[NSEC], margin)
    grid_rows = TILES // TCOLS
    return jnp.stack([padded[row_at * TH:row_at * TH + TH + 2 * margin, col_at * TW:col_at * TW + TW + 2 * margin] for row_at in range(grid_rows) for col_at in range(TCOLS)])


def setup_inputs(seed: int = 0) -> dict:
    arg_keys = jax.random.split(jax.random.key(seed), 3)
    return {
        "sections": draw_sections(jax.random.fold_in(arg_keys[2], 71), 0),
        "following": draw_following(jax.random.fold_in(arg_keys[2], 71), 0),
    }


sharpness = 128.0

def spectral_tables(length):
    counter = jnp.arange(length, dtype=jnp.int32)
    turn_index = counter[:, None] * counter[None, :] % length
    phase_angle = turn_index.astype(jnp.float32) * (2.0 * math.pi / length)
    return (jnp.cos(phase_angle).astype(jnp.bfloat16), jnp.sin(phase_angle).astype(jnp.bfloat16))

def full_product(left_matrix, operand):
    return jnp.einsum('ki,bim->bkm', left_matrix.astype(jnp.float32), operand.astype(jnp.float32), precision=lax.Precision.HIGHEST)

def split_spectrum(product, length):
    cos_cos = product[:, :length, :length]
    cos_sin = product[:, :length, length:]
    sin_cos = product[:, length:, :length]
    sin_sin = product[:, length:, length:]
    return ((cos_cos - sin_sin).astype(jnp.bfloat16), (-(sin_cos + cos_sin)).astype(jnp.bfloat16))

def spectrum(images, extent, cos_t, sin_t, multiply):
    batch_size = images.shape[0]
    length = cos_t.shape[0]
    right_table = jnp.concatenate([cos_t[:extent], sin_t[:extent]], 1)
    segment_one = jnp.dot(images.reshape(batch_size * extent, extent), right_table, preferred_element_type=jnp.float32)
    segment_one = segment_one.astype(jnp.bfloat16).reshape(batch_size, extent, 2 * length)
    left_table = jnp.concatenate([cos_t[:, :extent], sin_t[:, :extent]], 0)
    return split_spectrum(multiply(left_table, segment_one), length)

def soft_peak(scores, extent):
    highest = lax.optimization_barrier(jnp.max(scores, axis=(1, 2), keepdims=True))
    weight = jnp.exp(scores - highest)
    weight_sum = lax.optimization_barrier(jnp.sum(weight, axis=(1, 2)))
    offset = jnp.arange(extent, dtype=jnp.float32) - float(extent // 2)
    by_row = lax.optimization_barrier(jnp.sum(weight, axis=2))
    by_col = lax.optimization_barrier(jnp.sum(weight, axis=1))
    flow_rows = lax.optimization_barrier(jnp.sum(by_row * offset, axis=1)) / weight_sum
    flow_cols = lax.optimization_barrier(jnp.sum(by_col * offset, axis=1)) / weight_sum
    strength = (highest[:, 0, 0] + jnp.log(weight_sum)) / sharpness
    return (jnp.stack([flow_rows, flow_cols], 1), strength)

def correlate(patches, windows, multiply):
    batch_size = windows.shape[0]
    length = windows.shape[1]
    extent = patches.shape[1]
    cos_t, sin_t = spectral_tables(length)
    win_real, win_imag = spectrum(windows, length, cos_t, sin_t, multiply)
    pat_real, pat_imag = spectrum(patches, extent, cos_t, sin_t, multiply)
    pr32 = pat_real.astype(jnp.float32)
    pi32 = pat_imag.astype(jnp.float32)
    wr32 = win_real.astype(jnp.float32)
    wi32 = win_imag.astype(jnp.float32)
    cross_real = (pr32 * wr32 + pi32 * wi32).astype(jnp.bfloat16)
    cross_imag = (pr32 * wi32 - pi32 * wr32).astype(jnp.bfloat16)
    mixing = jnp.concatenate([jnp.concatenate([cos_t[:, :extent], sin_t[:, :extent]], 1), jnp.concatenate([-sin_t[:, :extent], cos_t[:, :extent]], 1)], 0)
    joined = jnp.concatenate([cross_real, cross_imag], 2).reshape(batch_size * length, 2 * length)
    returned = jnp.dot(joined, mixing, preferred_element_type=jnp.float32)
    returned = returned.astype(jnp.bfloat16).reshape(batch_size, length, 2 * extent)
    stacked = jnp.concatenate([returned[:, :, :extent], returned[:, :, extent:]], 1)
    final_table = jnp.concatenate([cos_t[:extent], -sin_t[:extent]], 1)
    correlation = multiply(final_table, stacked)
    scores = correlation * (sharpness / float(length * length * extent * extent))
    return soft_peak(scores, extent)

def standardize(images):
    centre = lax.optimization_barrier(jnp.mean(images, axis=(1, 2), keepdims=True))
    deviation = images - centre
    spread = lax.optimization_barrier(jnp.mean(deviation * deviation, axis=(1, 2), keepdims=True))
    return (deviation * lax.rsqrt(spread + 1e-05)).astype(jnp.bfloat16)

def cut_patches(strip_cells, extent, stride, batch_size):
    block_span = extent // stride
    blocks = strip_cells.reshape(extent, batch_size + block_span - 1, stride)
    gathered = jnp.concatenate([blocks[:, lead_block:lead_block + batch_size] for lead_block in range(block_span)], 2)
    return gathered.transpose(1, 0, 2)

def whole_section(tiles):
    grid_rows = TILES // TCOLS
    return tiles.reshape(grid_rows, TCOLS, TH, TW).transpose(0, 2, 1, 3).reshape(grid_rows * TH, TCOLS * TW)

def reference(sections, following):
    stride = PATCH // 2
    own_margin = PATCH // 4
    next_margin = 3 * PATCH // 4
    window = 2 * PATCH
    grid_rows = TILES // TCOLS
    centres = following[:, next_margin:next_margin + TH, next_margin:next_margin + TW]
    successors = jnp.concatenate([sections[1:], centres[None]], 0)
    patch_rows = grid_rows * TH // stride
    patch_cols = TCOLS * TW // stride

    def one_section(section_pair):
        current, upcoming = section_pair
        own_full = jnp.pad(whole_section(current), own_margin)
        next_full = jnp.pad(whole_section(upcoming), next_margin)

        def one_row(row_index):
            own_strip = lax.dynamic_slice_in_dim(own_full, row_index * stride, PATCH, 0)
            next_strip = lax.dynamic_slice_in_dim(next_full, row_index * stride, window, 0)
            patches = standardize(cut_patches(own_strip, PATCH, stride, patch_cols))
            windows = standardize(cut_patches(next_strip, window, stride, patch_cols))
            return correlate(patches, windows, full_product)
        flow_out, strength = lax.map(one_row, jnp.arange(patch_rows, dtype=jnp.int32))
        flow_out = flow_out.reshape(grid_rows, TH // stride, TCOLS, TW // stride, 2)
        flow_out = flow_out.transpose(0, 2, 4, 1, 3).reshape(TILES, 2, TH // stride * (TW // stride))
        strength = strength.reshape(grid_rows, TH // stride, TCOLS, TW // stride)
        strength = strength.transpose(0, 2, 1, 3).reshape(TILES, TH // stride * (TW // stride))
        return (flow_out, strength)
    flow, strength = lax.map(one_section, (sections, successors))
    return (flow, strength)
```

```python
import functools

import jax
import jax.numpy as jnp
import ml_dtypes
import numpy as np
from jax import lax
from jax.experimental import pallas as pl
from jax.experimental.pallas import tpu as pltpu
from jax.sharding import PartitionSpec as P

MESH = pl.DeviceIdType.MESH
F32 = jnp.float32
BF16 = jnp.bfloat16

PATCH = 128
WIN = 256
TH = 256
TW = 512
TCOLS = 4
TROWS = 4
SECS = 16
STRIDE = 64
WM = 96
PM = 32
LANE = 128
WROWS = TH + 2 * WM
PROWS = TH + 2 * PM
WIDE = TW + 2 * LANE
COUNT = 32


def table():
    b = np.arange(WIN)[:, None]
    turn = (b * (2 * np.arange(PATCH)[None, :] + 1)) % (2 * WIN)
    angle = turn * (np.pi / WIN)
    return np.concatenate([np.cos(angle), np.sin(angle)], 1).astype(np.float32).astype(ml_dtypes.bfloat16)


def standard(x):
    size = float(x.shape[0] * x.shape[1])
    centre = jnp.sum(x, keepdims=True) * (1.0 / size)
    deviation = x - centre
    spread = jnp.sum(deviation * deviation, keepdims=True) * (1.0 / size)
    return (deviation * lax.rsqrt(spread + 1e-5)).astype(BF16)


def dot(a, b):
    return jnp.dot(a, b, preferred_element_type=F32)


def four(z):
    p, r = z[:PATCH, :PATCH], z[:PATCH, PATCH:]
    t, q = z[PATCH:, :PATCH], z[PATCH:, PATCH:]
    return p - q, r + t, p + q, r - t


def window_spectrum(x, tc, tr):
    wa = dot(standard(x), tc).astype(BF16)
    return four(dot(tr, wa))


def patch_scores(x, g, tc, tr):
    pa = dot(standard(x), tc[:PATCH, :]).astype(BF16)
    f = [v.astype(BF16).astype(F32) for v in four(dot(tr[:, :PATCH], pa))]
    g = [v.astype(F32) for v in g]
    xr = f[0] * g[0] + f[1] * g[1]
    xi = f[1] * g[0] - f[0] * g[1]
    yr = f[2] * g[2] + f[3] * g[3]
    yi = f[3] * g[2] - f[2] * g[3]
    upper = jnp.concatenate([(xr + yr).astype(BF16), (-(xi + yi)).astype(BF16)], 1)
    lower = jnp.concatenate([(yi - xi).astype(BF16), (yr - xr).astype(BF16)], 1)
    back = dot(tc[:PATCH, :], jnp.concatenate([upper, lower], 0)).astype(BF16)
    return dot(back, tr[:, :PATCH]) * (1.0 / (32768.0 * 128.0))


def kernel(sec_ref, fol_ref, tc_ref, tr_ref, flow_ref, strength_ref,
           wx, px, fx, e_win, e_pat, spec, peak, res, res_in, lsem, wsend, wrecv, psend, precv, rsem):
    s, t = lax.axis_index("sec"), lax.axis_index("tile")
    r, c = t // TCOLS, lax.rem(t, TCOLS)
    after, before = lax.rem(s + 1, SECS), lax.rem(s + SECS - 1, SECS)
    has_up, has_down, has_left, has_right = r > 0, r < TROWS - 1, c > 0, c < TCOLS - 1
    up, down, left, right = (s, t - TCOLS), (s, t + TCOLS), (s, t - 1), (s, t + 1)
    first = s == 0
    sides = [(has_left, left), (has_right, right), (has_up, up), (has_down, down)]

    barrier = pltpu.get_barrier_semaphore()
    for d in ((after, t), (before, t)):
        pl.semaphore_signal(barrier, inc=1, device_id=d, device_id_type=MESH)
    for ok, d in sides:
        @pl.when(ok)
        def _():
            pl.semaphore_signal(barrier, inc=1, device_id=d, device_id_type=MESH)
    near = sum(ok.astype(jnp.int32) for ok, _ in sides)
    pl.semaphore_wait(barrier, 2 + near)

    def remote(src, dst, ssem, rsem, d):
        return pltpu.make_async_remote_copy(src_ref=src, dst_ref=dst, send_sem=ssem, recv_sem=rsem,
                                            device_id=d, device_id_type=MESH)

    own = sec_ref.at[0, 0]
    far = remote(own, px.at[pl.ds(PM, TH), pl.ds(LANE, TW)], psend.at[0], precv.at[0], (after, t))
    far.start()

    edge = TW - LANE
    wcols = [
        (has_left, has_right, remote(own.at[:, pl.ds(0, LANE)], wx.at[pl.ds(WM, TH), pl.ds(LANE + TW, LANE)], wsend.at[0], wrecv.at[0], left)),
        (has_right, has_left, remote(own.at[:, pl.ds(edge, LANE)], wx.at[pl.ds(WM, TH), pl.ds(0, LANE)], wsend.at[1], wrecv.at[1], right)),
    ]
    wrows = [
        (has_up, has_down, remote(own.at[pl.ds(0, WM)], wx.at[pl.ds(WM + TH, WM), pl.ds(LANE, TW)], wsend.at[2], wrecv.at[2], up)),
        (has_down, has_up, remote(own.at[pl.ds(TH - WM, WM)], wx.at[pl.ds(0, WM), pl.ds(LANE, TW)], wsend.at[3], wrecv.at[3], down)),
    ]

    def corners(buf, m, ssem, rsem, base):
        out = []
        for i, (side, lane) in enumerate(((has_left, 0), (has_right, LANE + TW))):
            lanes = pl.ds(lane, LANE)
            out.append((side & has_up, side & has_down, remote(
                buf.at[pl.ds(m, m), lanes], buf.at[pl.ds(m + TH, m), lanes], ssem.at[base + 2 * i], rsem.at[base + 2 * i], up)))
            out.append((side & has_down, side & has_up, remote(
                buf.at[pl.ds(TH, m), lanes], buf.at[pl.ds(0, m), lanes], ssem.at[base + 2 * i + 1], rsem.at[base + 2 * i + 1], down)))
        return out

    wcorners = corners(wx, WM, wsend, wrecv, 4)

    def start(copies):
        for ok, _, copy in copies:
            @pl.when(ok)
            def _():
                copy.start()

    def wait_recv(copies):
        for _, ok, copy in copies:
            @pl.when(ok)
            def _():
                copy.wait_recv()

    def wait_send(copies):
        for ok, _, copy in copies:
            @pl.when(ok)
            def _():
                copy.wait_send()

    @pl.when(jnp.logical_not(first))
    def _():
        start(wcols)
        start(wrows)

    centre = pltpu.make_async_copy(own, wx.at[pl.ds(WM, TH), pl.ds(LANE, TW)], lsem.at[0])
    spare = pltpu.make_async_copy(fol_ref.at[0], fx, lsem.at[0])

    @pl.when(jnp.logical_not(first))
    def _():
        centre.start()

    @pl.when(first)
    def _():
        spare.start()

    for buf, m in ((wx, WM), (px, PM)):
        rows = TH + 2 * m

        @pl.when(jnp.logical_not(has_up))
        def _():
            buf[0:m, :] = jnp.zeros((m, WIDE), F32)

        @pl.when(jnp.logical_not(has_down))
        def _():
            buf[m + TH:, :] = jnp.zeros((m, WIDE), F32)

        @pl.when(jnp.logical_not(has_left))
        def _():
            buf[:, 0:LANE] = jnp.zeros((rows, LANE), F32)

        @pl.when(jnp.logical_not(has_right))
        def _():
            buf[:, LANE + TW:] = jnp.zeros((rows, LANE), F32)

    @pl.when(jnp.logical_not(first))
    def _():
        wait_recv(wcols)
        start(wcorners)
        wait_recv(wrows)
        wait_recv(wcorners)
        centre.wait()
        for k in range(2):
            lane = LANE - WM + STRIDE * k
            e_win[k] = wx[:, lane:lane + 640]
        wait_send(wcols)
        wait_send(wrows)
        wait_send(wcorners)

    @pl.when(first)
    def _():
        spare.wait()
        for k in range(2):
            e_win[k] = fx[:, STRIDE * k:STRIDE * k + 640]

    tc, tr = tc_ref[...], tr_ref[...]

    def window_step(n, carry):
        i, j = n // 4, lax.rem(n, 4)
        rows = pl.ds(pl.multiple_of(i * STRIDE, STRIDE), WIN)
        lanes = pl.ds(pl.multiple_of(j * LANE, LANE), WIN)
        for k in range(2):
            for m, g in enumerate(window_spectrum(e_win[k, rows, lanes], tc, tr)):
                spec[n, k, m] = g.astype(BF16)
        return carry

    lax.fori_loop(0, 16, window_step, 0)

    far.wait_recv()
    pcols = [
        (has_left, has_right, remote(px.at[pl.ds(PM, TH), pl.ds(LANE, LANE)], px.at[pl.ds(PM, TH), pl.ds(LANE + TW, LANE)], psend.at[1], precv.at[1], left)),
        (has_right, has_left, remote(px.at[pl.ds(PM, TH), pl.ds(TW, LANE)], px.at[pl.ds(PM, TH), pl.ds(0, LANE)], psend.at[2], precv.at[2], right)),
    ]
    prows = [
        (has_up, has_down, remote(px.at[pl.ds(PM, PM), pl.ds(LANE, TW)], px.at[pl.ds(PM + TH, PM), pl.ds(LANE, TW)], psend.at[3], precv.at[3], up)),
        (has_down, has_up, remote(px.at[pl.ds(TH, PM), pl.ds(LANE, TW)], px.at[pl.ds(0, PM), pl.ds(LANE, TW)], psend.at[4], precv.at[4], down)),
    ]
    pcorners = corners(px, PM, psend, precv, 5)
    start(pcols)
    start(prows)
    wait_recv(pcols)
    start(pcorners)
    wait_recv(prows)
    wait_recv(pcorners)
    for k in range(2):
        lane = LANE - PM + STRIDE * k
        e_pat[k] = px[:, lane:lane + TW]

    offset = lax.broadcasted_iota(jnp.int32, (PATCH // 8, 8, PATCH), 0) * 8 + lax.broadcasted_iota(jnp.int32, (PATCH // 8, 8, PATCH), 1)
    offset = (offset - PATCH // 2).astype(F32)

    def patch_step(n, carry):
        i, j = n // 4, lax.rem(n, 4)
        rows = pl.ds(pl.multiple_of(i * STRIDE, STRIDE), PATCH)
        lanes = pl.ds(pl.multiple_of(j * LANE, LANE), PATCH)
        for k in range(2):
            score = patch_scores(e_pat[k, rows, lanes], [spec[n, k, m] for m in range(4)], tc, tr)
            score = score.reshape(PATCH // 8, 8, PATCH)
            high = jnp.max(score, axis=0)
            weight = jnp.exp(score - high[None])
            peak[0, 2 * n + k] = high
            peak[1, 2 * n + k] = jnp.sum(weight, axis=0)
            peak[2, 2 * n + k] = jnp.sum(weight * offset, axis=0)
        return carry

    lax.fori_loop(0, 16, patch_step, 0)

    high = peak[0]
    top = jnp.max(jnp.max(high, axis=1, keepdims=True), axis=2, keepdims=True)
    scale = jnp.exp(high - top)
    weight = peak[1] * scale
    column = (lax.broadcasted_iota(jnp.int32, (COUNT, 8, LANE), 2) - PATCH // 2).astype(F32)

    def total(x):
        return jnp.sum(jnp.sum(x, axis=1, keepdims=True), axis=2, keepdims=True)

    whole = total(weight)
    by_row = total(peak[2] * scale) / whole
    by_col = total(weight * column) / whole
    strength = (top + jnp.log(whole)) * (1.0 / 128.0)
    place = lax.broadcasted_iota(jnp.int32, (COUNT, 1, LANE), 0) == lax.broadcasted_iota(jnp.int32, (COUNT, 1, LANE), 2)
    for k, v in enumerate((by_row, by_col, strength)):
        res[k:k + 1, :] = jnp.sum(jnp.where(place, v, 0.0), axis=0)

    back = remote(res, res_in, rsem.at[0], rsem.at[1], (before, t))
    back.start()
    far.wait_send()
    wait_send(pcols)
    wait_send(prows)
    wait_send(pcorners)
    back.wait()
    flow_ref[0, 0] = res_in[0:2, 0:COUNT]
    strength_ref[0] = res_in[2:3, 0:COUNT]


def solution(mesh):
    tc = table()

    def local(sections, following):
        dma = pltpu.SemaphoreType.DMA
        return pl.pallas_call(
            kernel,
            out_shape=(jax.ShapeDtypeStruct((1, 1, 2, COUNT), F32), jax.ShapeDtypeStruct((1, 1, COUNT), F32)),
            in_specs=[pl.BlockSpec(memory_space=pl.ANY)] * 2 + [pl.BlockSpec(memory_space=pltpu.VMEM)] * 2,
            out_specs=(pl.BlockSpec(memory_space=pltpu.VMEM),) * 2,
            scratch_shapes=[
                pltpu.VMEM((WROWS, WIDE), F32),
                pltpu.VMEM((PROWS, WIDE), F32),
                pltpu.VMEM((WROWS, TW + 2 * WM), F32),
                pltpu.VMEM((2, WROWS, 640), F32),
                pltpu.VMEM((2, PROWS, TW), F32),
                pltpu.VMEM((16, 2, 4, PATCH, PATCH), BF16),
                pltpu.VMEM((3, COUNT, 8, LANE), F32),
                pltpu.VMEM((8, LANE), F32),
                pltpu.VMEM((8, LANE), F32),
                dma((1,)), dma((8,)), dma((8,)), dma((9,)), dma((9,)), dma((2,)),
            ],
            compiler_params=pltpu.CompilerParams(collective_id=0, has_side_effects=True, vmem_limit_bytes=40 * 2**20),
            name="patch_flow",
        )(sections, following, jnp.asarray(tc), jnp.asarray(np.ascontiguousarray(tc.T)))

    return jax.shard_map(
        local,
        mesh=mesh,
        in_specs=(P("sec", "tile", None, None), P("tile", None, None)),
        out_specs=(P("sec", "tile", None, None), P("sec", "tile", None)),
        check_vma=False,
    )
```

```python
import jax
import jax.numpy as jnp
import ml_dtypes
import numpy as np
from jax import lax
from jax.experimental import pallas as pl
from jax.experimental.pallas import tpu as pltpu
from jax.sharding import PartitionSpec as P

MESH = pl.DeviceIdType.MESH
F32 = jnp.float32
BF16 = jnp.bfloat16

PATCH = 128
WIN = 256
TH = 256
TW = 512
TCOLS = 4
TROWS = 4
SECS = 16
STRIDE = 64
WM = 96
PM = 32
LANE = 128
WROWS = TH + 2 * WM
PROWS = TH + 2 * PM
WIDE = TW + 2 * LANE
SPAN = TW + 2 * WM
COUNT = 32
CUTS = 4


def tables():
    b = np.arange(WIN)[:, None]
    turn = (b * (2 * np.arange(PATCH)[None, :] + 1)) % (2 * WIN)
    angle = turn * (np.pi / WIN)
    tc = np.concatenate([np.cos(angle), np.sin(angle)], 1)
    cr, sr = tc[:PATCH, :PATCH].T, tc[:PATCH, PATCH:].T
    four = np.concatenate([np.concatenate(x, 1) for x in ((cr, -sr), (sr, cr), (cr, sr), (-sr, cr))], 0)
    return [np.ascontiguousarray(v).astype(np.float32).astype(ml_dtypes.bfloat16) for v in (tc, tc.T, four)]


def dot(a, b):
    return jnp.dot(a, b, preferred_element_type=F32)


def tree(x):
    rows = x.shape[0]
    while rows > 8:
        rows //= 2
        x = x[:rows] + x[rows:]
    for h in (4, 2, 1):
        x = x + pltpu.roll(x, h, 0)
    return x


def strip_moments(x):
    mean = tree(x) * (1.0 / STRIDE)
    dev = x.reshape(STRIDE // 8, 8, x.shape[1]) - mean[None]
    return mean, tree((dev * dev).reshape(x.shape))


def merge(mean, dev2, size, shift, axis):
    n = mean.shape[axis]
    other = pltpu.roll(mean, n - shift, axis)
    gap = mean - other
    return (mean + other) * 0.5, dev2 + pltpu.roll(dev2, n - shift, axis) + gap * gap * (0.5 * size), 2 * size


def moments(strips, extent):
    sub = lax.broadcasted_iota(jnp.int32, (8, strips[0].shape[1]), 0)
    mean = jnp.zeros(sub.shape, F32)
    dev2 = jnp.zeros(sub.shape, F32)
    for i, x in enumerate(strips):
        m, d = strip_moments(x)
        mean = jnp.where(sub == i, m, mean)
        dev2 = jnp.where(sub == i, d, dev2)
    size = float(STRIDE)
    h = 1
    while h < extent:
        mean, dev2, size = merge(mean, dev2, size, h, 1)
        h *= 2
    h = STRIDE
    while h < extent:
        mean, dev2, size = merge(mean, dev2, size, h // STRIDE, 0)
        h *= 2
    return mean, lax.rsqrt(dev2 * (1.0 / size) + 1e-5)


def spread_out(stat, out, base, rows=8):
    for j in range(8):
        lane = base + STRIDE * j
        out[j, 0:rows] = jnp.broadcast_to(stat[:rows, lane:lane + 1], (rows, LANE))


def window_row(i, e0, e1, cen, tc, tr, spec):
    rows = pl.ds(pl.multiple_of(i * STRIDE, STRIDE), WIN)
    for j in range(8):
        e = (e0, e1)[j % 2]
        x = (e[rows, pl.ds(LANE * (j // 2), WIN)] - cen[j, pl.ds(i, 1), 0:1]).astype(BF16)
        z = dot(tr[...], dot(x, tc[...]).astype(BF16))
        p, r = z[:PATCH, :PATCH], z[:PATCH, PATCH:]
        t, q = z[PATCH:, :PATCH], z[PATCH:, PATCH:]
        for m, g in enumerate((p - q, r + t, p + q, r - t)):
            spec[i * 4 + j // 2, m, :, pl.ds(LANE * (j % 2), LANE)] = g.astype(BF16)


def cross(f, g):
    f = [v.astype(F32) for v in f]
    g = [v.astype(F32) for v in g]
    xr = f[0] * g[0] + f[1] * g[1]
    xi = f[0] * g[1] - f[1] * g[0]
    yr = f[2] * g[2] + f[3] * g[3]
    yi = f[2] * g[3] - f[3] * g[2]
    return [v.astype(BF16) for v in (xr + yr, xi + yi, xi - yi, yr - xr)]


def patch_row(i, px, pcen, pinv, winv, tc, tr, t4, spec, peak):
    rows = pl.ds(STRIDE * i, PATCH)
    offset = lax.broadcasted_iota(jnp.int32, (PATCH // 8, 8, PATCH), 0) * 8
    offset = offset + lax.broadcasted_iota(jnp.int32, (PATCH // 8, 8, PATCH), 1)
    offset = (offset - PATCH // 2).astype(F32)
    band = px[rows, :]
    x = []
    for j in range(8):
        lane = LANE - PM + STRIDE * j
        x.append((band[:, lane:lane + PATCH] - pcen[j, i:i + 1, 0:1]).astype(BF16))
    a = dot(jnp.concatenate(x, 0), tc[:PATCH, :]).astype(BF16)
    fs = []
    for jj in range(4):
        e, o = a[256 * jj:256 * jj + 128], a[256 * jj + 128:256 * jj + 256]
        upper = jnp.concatenate([e[:, :LANE], o[:, :LANE]], 1)
        lower = jnp.concatenate([e[:, LANE:], o[:, LANE:]], 1)
        fs.append(dot(t4[...], jnp.concatenate([upper, lower], 0)).astype(BF16))
    lhs = []
    for jj in range(4):
        f = [fs[jj][LANE * m:LANE * m + LANE] for m in range(4)]
        ar, ai, di, dr = cross(f, [spec[i * 4 + jj, m] for m in range(4)])
        for k in range(2):
            h = slice(LANE * k, LANE * k + LANE)
            lhs += [jnp.concatenate([ar[:, h], ai[:, h]], 1), jnp.concatenate([di[:, h], dr[:, h]], 1)]
    uv = dot(jnp.concatenate(lhs, 0), tr[:, :PATCH]).astype(BF16)
    for jj in range(4):
        s = dot(tc[:PATCH, :], jnp.concatenate([uv[512 * jj:512 * jj + 256], uv[512 * jj + 256:512 * jj + 512]], 1))
        for k in range(2):
            j = 2 * jj + k
            scale = pinv[j, i:i + 1, :] * winv[j, i:i + 1, :] * (1.0 / (32768.0 * 128.0))
            score = (s[:, LANE * k:LANE * k + LANE] * scale).reshape(PATCH // 8, 8, PATCH)
            high = jnp.max(score, axis=0)
            weight = jnp.exp(score - high[None])
            peak[0, i * 8 + j] = high
            peak[1, i * 8 + j] = jnp.sum(weight, axis=0)
            peak[2, i * 8 + j] = jnp.sum(weight * offset, axis=0)


def finish(peak, res):
    high = peak[0]
    top = jnp.max(jnp.max(high, axis=1, keepdims=True), axis=2, keepdims=True)
    scale = jnp.exp(high - top)
    weight = peak[1] * scale
    column = (lax.broadcasted_iota(jnp.int32, (COUNT, 8, LANE), 2) - PATCH // 2).astype(F32)

    def total(x):
        return jnp.sum(jnp.sum(x, axis=1, keepdims=True), axis=2, keepdims=True)

    whole = total(weight)
    by_row = total(peak[2] * scale) / whole
    by_col = total(weight * column) / whole
    strength = (top + jnp.log(whole)) * (1.0 / 128.0)
    place = lax.broadcasted_iota(jnp.int32, (COUNT, 1, LANE), 0) == lax.broadcasted_iota(jnp.int32, (COUNT, 1, LANE), 2)
    for k, v in enumerate((by_row, by_col, strength)):
        res[k:k + 1, :] = jnp.sum(jnp.where(place, v, 0.0), axis=0)


def pack(x, lane):
    group = lax.broadcasted_iota(jnp.int32, (16, LANE), 1) // PM
    out = jnp.zeros((16, LANE), F32)
    for g in range(4):
        part = x[16 * g:16 * g + 16]
        shift = (PM * g - lane) % LANE
        out = jnp.where(group == g, pltpu.roll(part, shift, 1) if shift else part, out)
    return out


def unpack(y, lane):
    out = []
    for g in range(4):
        shift = (lane - PM * g) % LANE
        out.append(pltpu.roll(y, shift, 1) if shift else y)
    return jnp.concatenate(out, 0)


def when(ok):
    return pl.when(ok)


def kernel(sec_ref, fol_ref, tc_ref, tr_ref, t4_ref, flow_ref, strength_ref,
           tc, tr, t4, wx, px, e0, e1, wcen, winv, pcen, pinv, spec, peak, out_cols, in_cols, res, res_in,
           lsem, wsend, wrecv, fsend, frecv, psend, precv, csend, crecv, rsem):
    s, t = lax.axis_index("sec"), lax.axis_index("tile")
    r, c = t // TCOLS, lax.rem(t, TCOLS)
    after, before = lax.rem(s + 1, SECS), lax.rem(s + SECS - 1, SECS)
    has_up, has_down, has_left, has_right = r > 0, r < TROWS - 1, c > 0, c < TCOLS - 1
    up, down, left, right = (s, t - TCOLS), (s, t + TCOLS), (s, t - 1), (s, t + 1)
    first = s == 0
    inner = jnp.logical_not(first)
    sides = [(has_left, left), (has_right, right), (has_up, up), (has_down, down)]

    barrier = pltpu.get_barrier_semaphore()
    for d in ((after, t), (before, t)):
        pl.semaphore_signal(barrier, inc=1, device_id=d, device_id_type=MESH)
    for ok, d in sides:
        @when(ok)
        def _():
            pl.semaphore_signal(barrier, inc=1, device_id=d, device_id_type=MESH)

    own = sec_ref.at[0, 0]
    constants = [pltpu.make_async_copy(a, b, lsem.at[1 + n]) for n, (a, b) in enumerate(((tc_ref, tc), (tr_ref, tr), (t4_ref, t4)))]
    centre = pltpu.make_async_copy(own, wx.at[pl.ds(WM, TH), pl.ds(LANE, TW)], lsem.at[0])
    spare = pltpu.make_async_copy(fol_ref.at[0], e0, lsem.at[0])

    @when(inner)
    def _():
        centre.start()

    @when(first)
    def _():
        spare.start()

    for copy in constants:
        copy.start()

    for buf, m in ((wx, WM), (px, PM)):
        rows = TH + 2 * m

        @when(jnp.logical_not(has_up))
        def _():
            buf[0:m, :] = jnp.zeros((m, WIDE), F32)

        @when(jnp.logical_not(has_down))
        def _():
            buf[m + TH:, :] = jnp.zeros((m, WIDE), F32)

        @when(jnp.logical_not(has_left))
        def _():
            buf[:, 0:LANE] = jnp.zeros((rows, LANE), F32)

        @when(jnp.logical_not(has_right))
        def _():
            buf[:, LANE + TW:] = jnp.zeros((rows, LANE), F32)

    res[...] = jnp.zeros((8, LANE), F32)

    near = sum(ok.astype(jnp.int32) for ok, _ in sides)
    pl.semaphore_wait(barrier, 2 + near)

    def remote(src, dst, ssem, rsem, d):
        return pltpu.make_async_remote_copy(src_ref=src, dst_ref=dst, send_sem=ssem, recv_sem=rsem,
                                            device_id=d, device_id_type=MESH)

    def start(copies):
        for ok, _, copy in copies:
            @when(ok)
            def _():
                copy.start()

    def wait_recv(copies):
        for _, ok, copy in copies:
            @when(ok)
            def _():
                copy.wait_recv()

    def wait_send(copies):
        for ok, _, copy in copies:
            @when(ok)
            def _():
                copy.wait_send()

    edge = TW - LANE
    wcols = [
        (has_left, has_right, remote(own.at[:, pl.ds(0, LANE)], wx.at[pl.ds(WM, TH), pl.ds(LANE + TW, LANE)], wsend.at[0], wrecv.at[0], left)),
        (has_right, has_left, remote(own.at[:, pl.ds(edge, LANE)], wx.at[pl.ds(WM, TH), pl.ds(0, LANE)], wsend.at[1], wrecv.at[1], right)),
    ]
    wrows = [
        (has_up, has_down, remote(own.at[pl.ds(0, WM)], wx.at[pl.ds(WM + TH, WM), pl.ds(LANE, TW)], wsend.at[2], wrecv.at[2], up)),
        (has_down, has_up, remote(own.at[pl.ds(TH - WM, WM)], wx.at[pl.ds(0, WM), pl.ds(LANE, TW)], wsend.at[3], wrecv.at[3], down)),
    ]

    def corners(buf, m, ssem, rsem, base):
        out = []
        for i, (side, lane) in enumerate(((has_left, 0), (has_right, LANE + TW))):
            lanes = pl.ds(lane, LANE)
            out.append((side & has_up, side & has_down, remote(
                buf.at[pl.ds(m, m), lanes], buf.at[pl.ds(m + TH, m), lanes], ssem.at[base + 2 * i], rsem.at[base + 2 * i], up)))
            out.append((side & has_down, side & has_up, remote(
                buf.at[pl.ds(TH, m), lanes], buf.at[pl.ds(0, m), lanes], ssem.at[base + 2 * i + 1], rsem.at[base + 2 * i + 1], down)))
        return out

    wcorners = corners(wx, WM, wsend, wrecv, 4)

    ranges = [(0, PM), (TH - PM, PM)] + [(PM + STRIDE * n, STRIDE) for n in range(CUTS - 1)]
    far = [remote(own.at[pl.ds(a, n)], px.at[pl.ds(PM + a, n), pl.ds(LANE, TW)], fsend.at[k], frecv.at[k], (after, t))
           for k, (a, n) in enumerate(ranges)]

    @when(inner)
    def _():
        start(wcols)
        start(wrows)

    for copy in far:
        copy.start()

    prows = [
        (has_up, has_down, remote(px.at[pl.ds(PM, PM), pl.ds(LANE, TW)], px.at[pl.ds(PM + TH, PM), pl.ds(LANE, TW)], psend.at[0], precv.at[0], up)),
        (has_down, has_up, remote(px.at[pl.ds(TH, PM), pl.ds(LANE, TW)], px.at[pl.ds(0, PM), pl.ds(LANE, TW)], psend.at[1], precv.at[1], down)),
    ]
    pcorners = corners(px, PM, psend, precv, 2)
    pcols = [[
        (has_left, has_right, remote(out_cols.at[2 * n], in_cols.at[2 * n], csend.at[2 * n], crecv.at[2 * n], left)),
        (has_right, has_left, remote(out_cols.at[2 * n + 1], in_cols.at[2 * n + 1], csend.at[2 * n + 1], crecv.at[2 * n + 1], right)),
    ] for n in range(CUTS)]

    def part(n):
        if n == 0:
            return [(PM, PM), (TH, PM)]
        return [(STRIDE * n, STRIDE)]

    def send_cols(n):
        for side, (ok, lane, at) in enumerate(((has_left, LANE, 0), (has_right, TW, LANE - PM))):
            @when(ok)
            def _():
                x = jnp.concatenate([px[a:a + m, lane:lane + LANE] for a, m in part(n)], 0)
                out_cols[2 * n + side] = pack(x, at)
        start(pcols[n])

    def take_cols(n):
        wait_recv(pcols[n])
        for side, (ok, lane, at) in enumerate(((has_right, LANE + TW, 0), (has_left, 0, LANE - PM))):
            @when(ok)
            def _():
                y = unpack(in_cols[2 * n + side], at)
                b = 0
                for a, m in part(n):
                    px[a:a + m, lane:lane + LANE] = y[b:b + m]
                    b += m

    @when(inner)
    def _():
        wait_recv(wcols)
        start(wcorners)

    for k in range(2):
        far[k].wait_recv()
    start(prows)
    send_cols(0)

    @when(inner)
    def _():
        wait_recv(wrows)
        wait_recv(wcorners)
        centre.wait()
        e0[...] = wx[:, LANE - WM:LANE - WM + SPAN]

    @when(first)
    def _():
        spare.wait()

    e1[...] = e0[:, STRIDE:]
    mean, inverse = moments(
        [jnp.concatenate([e0[STRIDE * i:STRIDE * i + STRIDE, :], jnp.zeros((STRIDE, WIDE - SPAN), F32)], 1) for i in range(7)], WIN)
    spread_out(mean, wcen, 0)
    spread_out(inverse, winv, 0)

    take_cols(0)
    start(pcorners)
    for copy in constants:
        copy.wait()

    def window_step(i, carry):
        window_row(i, e0, e1, wcen, tc, tr, spec)
        return carry

    lax.fori_loop(0, 4, window_step, 0)

    for n in range(1, CUTS):
        far[n + 1].wait_recv()
        send_cols(n)
        if n > 1:
            take_cols(n - 1)
    wait_recv(prows)
    wait_recv(pcorners)
    take_cols(CUTS - 1)
    mean, inverse = moments([px[STRIDE * i:STRIDE * i + STRIDE, :] for i in range(5)], PATCH)
    spread_out(mean, pcen, LANE - PM)
    spread_out(inverse, pinv, LANE - PM)
    for i in range(4):
        patch_row(i, px, pcen, pinv, winv, tc, tr, t4, spec, peak)
    finish(peak, res)
    back = remote(res, res_in, rsem.at[0], rsem.at[1], (before, t))
    back.start()

    @when(inner)
    def _():
        wait_send(wcols)
        wait_send(wrows)
        wait_send(wcorners)

    for copy in far:
        copy.wait_send()
    wait_send(prows)
    wait_send(pcorners)
    for copies in pcols:
        wait_send(copies)
    back.wait()
    flow_ref[0, 0] = res_in[0:2, 0:COUNT]
    strength_ref[0] = res_in[2:3, 0:COUNT]


def solution(mesh):
    tabs = tables()

    def local(sections, following):
        dma = pltpu.SemaphoreType.DMA
        vmem = pltpu.VMEM
        return pl.pallas_call(
            kernel,
            out_shape=(jax.ShapeDtypeStruct((1, 1, 2, COUNT), F32), jax.ShapeDtypeStruct((1, 1, COUNT), F32)),
            in_specs=[pl.BlockSpec(memory_space=pl.ANY)] * 5,
            out_specs=(pl.BlockSpec(memory_space=vmem),) * 2,
            scratch_shapes=[
                vmem((WIN, WIN), BF16), vmem((WIN, WIN), BF16), vmem((2 * WIN, WIN), BF16),
                vmem((WROWS, WIDE), F32),
                vmem((PROWS, WIDE), F32),
                vmem((WROWS, SPAN), F32),
                vmem((WROWS, SPAN - STRIDE), F32),
                vmem((8, 8, LANE), F32), vmem((8, 8, LANE), F32), vmem((8, 8, LANE), F32), vmem((8, 8, LANE), F32),
                vmem((16, 4, PATCH, WIN), BF16),
                vmem((3, COUNT, 8, LANE), F32),
                vmem((2 * CUTS, 16, LANE), F32),
                vmem((2 * CUTS, 16, LANE), F32),
                vmem((8, LANE), F32),
                vmem((8, LANE), F32),
                dma((4,)), dma((8,)), dma((8,)), dma((CUTS + 1,)), dma((CUTS + 1,)),
                dma((6,)), dma((6,)), dma((2 * CUTS,)), dma((2 * CUTS,)), dma((2,)),
            ],
            compiler_params=pltpu.CompilerParams(collective_id=0, has_side_effects=True, vmem_limit_bytes=58 * 2**20),
            name="patch_flow",
        )(sections, following, *[jnp.asarray(v) for v in tabs])

    return jax.shard_map(
        local,
        mesh=mesh,
        in_specs=(P("sec", "tile", None, None), P("tile", None, None)),
        out_specs=(P("sec", "tile", None, None), P("sec", "tile", None)),
        check_vma=False,
    )
```

```python
import jax
import jax.numpy as jnp
import ml_dtypes
import numpy as np
from jax import lax
from jax.experimental import pallas as pl
from jax.experimental.pallas import tpu as pltpu
from jax.sharding import PartitionSpec as P

MESH = pl.DeviceIdType.MESH
F32 = jnp.float32
BF16 = jnp.bfloat16

PATCH = 128
WIN = 256
TH = 256
TW = 512
TCOLS = 4
TROWS = 4
SECS = 16
STRIDE = 64
WM = 96
PM = 32
LANE = 128
WROWS = TH + 2 * WM
PROWS = TH + 2 * PM
WIDE = TW + 2 * LANE
SPAN = TW + 2 * WM
COUNT = 32
CUTS = 4


def tables():
    b = np.arange(WIN)[:, None]
    turn = (b * (2 * np.arange(PATCH)[None, :] + 1)) % (2 * WIN)
    angle = turn * (np.pi / WIN)
    tc = np.concatenate([np.cos(angle), np.sin(angle)], 1)
    cr, sr = tc[:PATCH, :PATCH].T, tc[:PATCH, PATCH:].T
    four = np.concatenate([np.concatenate(x, 1) for x in ((cr, -sr), (sr, cr), (cr, sr), (-sr, cr))], 0)
    return [np.ascontiguousarray(v).astype(np.float32).astype(ml_dtypes.bfloat16) for v in (tc, tc.T, four)]


def dot(a, b):
    return jnp.dot(a, b, preferred_element_type=F32)


def tree(x):
    rows = x.shape[0]
    while rows > 8:
        rows //= 2
        x = x[:rows] + x[rows:]
    for h in (4, 2, 1):
        x = x + pltpu.roll(x, h, 0)
    return x


def strip_moments(x):
    mean = tree(x) * (1.0 / STRIDE)
    dev = x.reshape(STRIDE // 8, 8, x.shape[1]) - mean[None]
    return mean, tree((dev * dev).reshape(x.shape))


def merge(mean, dev2, size, shift, axis):
    n = mean.shape[axis]
    other = pltpu.roll(mean, n - shift, axis)
    gap = mean - other
    return (mean + other) * 0.5, dev2 + pltpu.roll(dev2, n - shift, axis) + gap * gap * (0.5 * size), 2 * size


def moments(strips, extent):
    sub = lax.broadcasted_iota(jnp.int32, (8, strips[0].shape[1]), 0)
    mean = jnp.zeros(sub.shape, F32)
    dev2 = jnp.zeros(sub.shape, F32)
    for i, x in enumerate(strips):
        m, d = strip_moments(x)
        mean = jnp.where(sub == i, m, mean)
        dev2 = jnp.where(sub == i, d, dev2)
    size = float(STRIDE)
    h = 1
    while h < extent:
        mean, dev2, size = merge(mean, dev2, size, h, 1)
        h *= 2
    h = STRIDE
    while h < extent:
        mean, dev2, size = merge(mean, dev2, size, h // STRIDE, 0)
        h *= 2
    return mean, lax.rsqrt(dev2 * (1.0 / size) + 1e-5)


def spread_out(stat, out, base, rows=8):
    for j in range(8):
        lane = base + STRIDE * j
        out[j, 0:rows] = jnp.broadcast_to(stat[:rows, lane:lane + 1], (rows, LANE))


def window_row(i, e0, e1, cen, tc, tr, spec):
    rows = pl.ds(pl.multiple_of(i * STRIDE, STRIDE), WIN)
    for j in range(8):
        e = (e0, e1)[j % 2]
        x = (e[rows, pl.ds(LANE * (j // 2), WIN)] - cen[j, pl.ds(i, 1), 0:1]).astype(BF16)
        z = dot(tr[...], dot(x, tc[...]).astype(BF16))
        p, r = z[:PATCH, :PATCH], z[:PATCH, PATCH:]
        t, q = z[PATCH:, :PATCH], z[PATCH:, PATCH:]
        for m, g in enumerate((p - q, r + t, p + q, r - t)):
            spec[i * 4 + j // 2, m, :, pl.ds(LANE * (j % 2), LANE)] = g.astype(BF16)


def cross(f, g):
    f = [v.astype(F32) for v in f]
    g = [v.astype(F32) for v in g]
    xr = f[0] * g[0] + f[1] * g[1]
    xi = f[0] * g[1] - f[1] * g[0]
    yr = f[2] * g[2] + f[3] * g[3]
    yi = f[2] * g[3] - f[3] * g[2]
    return [v.astype(BF16) for v in (xr + yr, xi + yi, xi - yi, yr - xr)]


def patch_moments(px, slot, base, pcen, pinv):
    strips = [px[slot, pl.ds(pl.multiple_of(base + STRIDE * i, STRIDE), STRIDE), :] for i in range(3)]
    mean, inverse = moments(strips, PATCH)
    spread_out(mean, pcen, LANE - PM)
    spread_out(inverse, pinv, LANE - PM)


def patch_row(i, px, slot, m, pcen, pinv, winv, tc, tr, t4, spec, peak):
    offset = lax.broadcasted_iota(jnp.int32, (PATCH // 8, 8, PATCH), 0) * 8
    offset = offset + lax.broadcasted_iota(jnp.int32, (PATCH // 8, 8, PATCH), 1)
    offset = (offset - PATCH // 2).astype(F32)
    band = px[slot, pl.ds(pl.multiple_of(STRIDE * i, STRIDE), PATCH), :]
    at, one = pl.ds(m, 1), pl.ds(i, 1)
    x = []
    for j in range(8):
        lane = LANE - PM + STRIDE * j
        x.append((band[:, lane:lane + PATCH] - pcen[j, at, 0:1]).astype(BF16))
    a = dot(jnp.concatenate(x, 0), tc[:PATCH, :]).astype(BF16)
    fs = []
    for jj in range(4):
        e, o = a[256 * jj:256 * jj + 128], a[256 * jj + 128:256 * jj + 256]
        upper = jnp.concatenate([e[:, :LANE], o[:, :LANE]], 1)
        lower = jnp.concatenate([e[:, LANE:], o[:, LANE:]], 1)
        fs.append(dot(t4[...], jnp.concatenate([upper, lower], 0)).astype(BF16))
    lhs = []
    for jj in range(4):
        f = [fs[jj][LANE * n:LANE * n + LANE] for n in range(4)]
        ar, ai, di, dr = cross(f, [spec[i * 4 + jj, n] for n in range(4)])
        for k in range(2):
            h = slice(LANE * k, LANE * k + LANE)
            lhs += [jnp.concatenate([ar[:, h], ai[:, h]], 1), jnp.concatenate([di[:, h], dr[:, h]], 1)]
    uv = dot(jnp.concatenate(lhs, 0), tr[:, :PATCH]).astype(BF16)
    for jj in range(4):
        s = dot(tc[:PATCH, :], jnp.concatenate([uv[512 * jj:512 * jj + 256], uv[512 * jj + 256:512 * jj + 512]], 1))
        for k in range(2):
            j = 2 * jj + k
            scale = pinv[j, at, :] * winv[j, one, :] * (1.0 / (32768.0 * 128.0))
            score = (s[:, LANE * k:LANE * k + LANE] * scale).reshape(PATCH // 8, 8, PATCH)
            high = jnp.max(score, axis=0)
            weight = jnp.exp(score - high[None])
            peak[0, i * 8 + j] = high
            peak[1, i * 8 + j] = jnp.sum(weight, axis=0)
            peak[2, i * 8 + j] = jnp.sum(weight * offset, axis=0)


def finish(peak, res, slot):
    high = peak[0]
    top = jnp.max(jnp.max(high, axis=1, keepdims=True), axis=2, keepdims=True)
    scale = jnp.exp(high - top)
    weight = peak[1] * scale
    column = (lax.broadcasted_iota(jnp.int32, (COUNT, 8, LANE), 2) - PATCH // 2).astype(F32)

    def total(x):
        return jnp.sum(jnp.sum(x, axis=1, keepdims=True), axis=2, keepdims=True)

    whole = total(weight)
    by_row = total(peak[2] * scale) / whole
    by_col = total(weight * column) / whole
    strength = (top + jnp.log(whole)) * (1.0 / 128.0)
    place = lax.broadcasted_iota(jnp.int32, (COUNT, 1, LANE), 0) == lax.broadcasted_iota(jnp.int32, (COUNT, 1, LANE), 2)
    for k, v in enumerate((by_row, by_col, strength)):
        res[slot, k:k + 1, :] = jnp.sum(jnp.where(place, v, 0.0), axis=0)


def pack(x, lane):
    group = lax.broadcasted_iota(jnp.int32, (16, LANE), 1) // PM
    out = jnp.zeros((16, LANE), F32)
    for g in range(4):
        part = x[16 * g:16 * g + 16]
        shift = (PM * g - lane) % LANE
        out = jnp.where(group == g, pltpu.roll(part, shift, 1) if shift else part, out)
    return out


def unpack(y, lane):
    out = []
    for g in range(4):
        shift = (lane - PM * g) % LANE
        out.append(pltpu.roll(y, shift, 1) if shift else y)
    return jnp.concatenate(out, 0)


def when(ok):
    return pl.when(ok)


def kernel(sec_ref, fol_ref, tc_ref, tr_ref, t4_ref, out_ref,
           tc, tr, t4, wx, px, e0, e1, wcen, winv, pcen, pinv, spec, peak, out_cols, in_cols, res, res_in,
           lsem, wsend, wrecv, fsend, frecv, psend, precv, csend, crecv, rsem, grant_sem):
    s, t = lax.axis_index("sec"), lax.axis_index("tile")
    r, c = t // TCOLS, lax.rem(t, TCOLS)
    after, before = lax.rem(s + 1, SECS), lax.rem(s + SECS - 1, SECS)
    has_up, has_down, has_left, has_right = r > 0, r < TROWS - 1, c > 0, c < TCOLS - 1
    up, down, left, right = (s, t - TCOLS), (s, t + TCOLS), (s, t - 1), (s, t + 1)
    first, last = s == 0, s == SECS - 1
    inner = s > 0
    even = lax.rem(s, 2) == 0
    odd = jnp.logical_not(even)
    taker = even & inner
    sender = odd & jnp.logical_not(last)
    eager = lax.rem(s // 2, 2) == 1
    sides = [(has_left, left), (has_right, right), (has_up, up), (has_down, down)]
    near = sum(ok.astype(jnp.int32) for ok, _ in sides)

    barrier = pltpu.get_barrier_semaphore()

    def signal(sem, d):
        pl.semaphore_signal(sem, inc=1, device_id=d, device_id_type=MESH)

    evens = jnp.where(even, s, before)
    for (ok, _), step in zip(sides, (-1, 1, -TCOLS, TCOLS)):
        @when(ok)
        def _():
            signal(barrier, (evens, t + step))

    @when(inner)
    def _():
        signal(barrier, (before, t))

    own = sec_ref.at[0, 0]
    constants = [pltpu.make_async_copy(a, b, lsem.at[2 + n]) for n, (a, b) in enumerate(((tc_ref, tc), (tr_ref, tr), (t4_ref, t4)))]
    centre = pltpu.make_async_copy(own, wx.at[pl.ds(WM, TH), pl.ds(LANE, TW)], lsem.at[0])
    spare = pltpu.make_async_copy(fol_ref.at[0], e0, lsem.at[1])
    centre.start()

    @when(last)
    def _():
        spare.start()

    for copy in constants:
        copy.start()

    def clear(buf, at, m):
        rows = TH + 2 * m

        @when(jnp.logical_not(has_up))
        def _():
            buf[at + (pl.ds(0, m), slice(None))] = jnp.zeros((m, WIDE), F32)

        @when(jnp.logical_not(has_down))
        def _():
            buf[at + (pl.ds(m + TH, m), slice(None))] = jnp.zeros((m, WIDE), F32)

        @when(jnp.logical_not(has_left))
        def _():
            buf[at + (slice(None), pl.ds(0, LANE))] = jnp.zeros((rows, LANE), F32)

        @when(jnp.logical_not(has_right))
        def _():
            buf[at + (slice(None), pl.ds(LANE + TW, LANE))] = jnp.zeros((rows, LANE), F32)

    clear(wx, (), WM)

    @when(taker)
    def _():
        clear(px, (0,), PM)

    res[...] = jnp.zeros(res.shape, F32)

    @when(even)
    def _():
        pl.semaphore_wait(barrier, 2 * near + 1)

        @when(jnp.logical_not(eager))
        def _():
            signal(grant_sem, (after, t))

    def remote(src, dst, ssem, rsem, d):
        return pltpu.make_async_remote_copy(src_ref=src, dst_ref=dst, send_sem=ssem, recv_sem=rsem,
                                            device_id=d, device_id_type=MESH)

    def start(copies):
        for ok, _, copy in copies:
            @when(ok)
            def _():
                copy.start()

    def wait_recv(copies):
        for _, ok, copy in copies:
            @when(ok)
            def _():
                copy.wait_recv()

    def wait_send(copies):
        for ok, _, copy in copies:
            @when(ok)
            def _():
                copy.wait_send()

    edge = TW - LANE
    wcols = [
        (has_left, has_right, remote(own.at[:, pl.ds(0, LANE)], wx.at[pl.ds(WM, TH), pl.ds(LANE + TW, LANE)], wsend.at[0], wrecv.at[0], left)),
        (has_right, has_left, remote(own.at[:, pl.ds(edge, LANE)], wx.at[pl.ds(WM, TH), pl.ds(0, LANE)], wsend.at[1], wrecv.at[1], right)),
    ]
    wrows = [
        (has_up, has_down, remote(own.at[pl.ds(0, WM)], wx.at[pl.ds(WM + TH, WM), pl.ds(LANE, TW)], wsend.at[2], wrecv.at[2], up)),
        (has_down, has_up, remote(own.at[pl.ds(TH - WM, WM)], wx.at[pl.ds(0, WM), pl.ds(LANE, TW)], wsend.at[3], wrecv.at[3], down)),
    ]

    def corners(buf, at, m, ssem, rsem, base):
        out = []
        for i, (side, lane) in enumerate(((has_left, 0), (has_right, LANE + TW))):
            def rows(a):
                return buf.at[at + (pl.ds(a, m), pl.ds(lane, LANE))]
            out.append((side & has_up, side & has_down, remote(
                rows(m), rows(m + TH), ssem.at[base + 2 * i], rsem.at[base + 2 * i], up)))
            out.append((side & has_down, side & has_up, remote(
                rows(TH), rows(0), ssem.at[base + 2 * i + 1], rsem.at[base + 2 * i + 1], down)))
        return out

    wcorners = corners(wx, (), WM, wsend, wrecv, 4)

    ranges = [(0, PM), (TH - PM, PM)] + [(PM + STRIDE * n, STRIDE) for n in range(CUTS - 1)]
    far = [remote(own.at[pl.ds(a, n)], px.at[0, pl.ds(PM + a, n), pl.ds(LANE, TW)], fsend.at[k], frecv.at[k], (after, t))
           for k, (a, n) in enumerate(ranges)]
    whole = remote(wx.at[pl.ds(WM - PM, PROWS)], px.at[0], fsend.at[CUTS + 1], frecv.at[CUTS + 1], (after, t))

    def first_margins():
        start(wcols)
        start(wrows)

    def far_start(copies):
        @when(sender)
        def _():
            for copy in copies:
                copy.start()

    def far_permission():
        @when(sender)
        def _():
            pl.semaphore_wait(barrier, 1)

    def second_margins():
        wait_recv(wcols)
        start(wcorners)

    @when(even)
    def _():
        first_margins()
        second_margins()

        @when(eager)
        def _():
            signal(grant_sem, (after, t))

    @when(odd & eager)
    def _():
        far_permission()
        far_start(far[:3])
        pl.semaphore_wait(grant_sem, 1)
        first_margins()
        far_start(far[3:])
        second_margins()

    @when(odd & jnp.logical_not(eager))
    def _():
        pl.semaphore_wait(grant_sem, 1)
        first_margins()
        far_permission()
        far_start(far)
        second_margins()

    prows = [
        (has_up, has_down, remote(px.at[0, pl.ds(PM, PM), pl.ds(LANE, TW)], px.at[0, pl.ds(PM + TH, PM), pl.ds(LANE, TW)], psend.at[0], precv.at[0], up)),
        (has_down, has_up, remote(px.at[0, pl.ds(TH, PM), pl.ds(LANE, TW)], px.at[0, pl.ds(0, PM), pl.ds(LANE, TW)], psend.at[1], precv.at[1], down)),
    ]
    pcorners = corners(px, (0,), PM, psend, precv, 2)
    pcols = [[
        (has_left, has_right, remote(out_cols.at[2 * n], in_cols.at[2 * n], csend.at[2 * n], crecv.at[2 * n], left)),
        (has_right, has_left, remote(out_cols.at[2 * n + 1], in_cols.at[2 * n + 1], csend.at[2 * n + 1], crecv.at[2 * n + 1], right)),
    ] for n in range(CUTS)]

    def part(n):
        if n == 0:
            return [(PM, PM), (TH, PM)]
        return [(STRIDE * n, STRIDE)]

    def send_cols(n):
        for side, (ok, lane, at) in enumerate(((has_left, LANE, 0), (has_right, TW, LANE - PM))):
            @when(ok)
            def _():
                x = jnp.concatenate([px[0, a:a + m, lane:lane + LANE] for a, m in part(n)], 0)
                out_cols[2 * n + side] = pack(x, at)
        start(pcols[n])

    def take_cols(n):
        wait_recv(pcols[n])
        for side, (ok, lane, at) in enumerate(((has_right, LANE + TW, 0), (has_left, 0, LANE - PM))):
            @when(ok)
            def _():
                y = unpack(in_cols[2 * n + side], at)
                b = 0
                for a, m in part(n):
                    px[0, a:a + m, lane:lane + LANE] = y[b:b + m]
                    b += m

    def far_take(n):
        for k in ((0, 1) if n == 0 else (n + 1,)):
            far[k].wait_recv()
        if n == 0:
            start(prows)
        send_cols(n)

    for copy in constants:
        copy.wait()
    centre.wait()

    @when(taker)
    def _():
        far_take(0)

    def extended():
        wait_recv(wrows)
        wait_recv(wcorners)

        @when(even)
        def _():
            whole.start()

    @when(first)
    def _():
        extended()

    back = remote(res.at[1], res_in, rsem.at[0], rsem.at[1], (before, t))

    def work(n, carry):
        @when(n == 0)
        def _():
            spare.wait()

        @when((n == 1) & jnp.logical_not(last))
        def _():
            extended()

        @when(n == 1)
        def _():
            e0[...] = wx[:, LANE - WM:LANE - WM + SPAN]

        e1[...] = e0[:, STRIDE:]
        mean, inverse = moments(
            [jnp.concatenate([e0[STRIDE * i:STRIDE * i + STRIDE, :], jnp.zeros((STRIDE, WIDE - SPAN), F32)], 1) for i in range(7)], WIN)
        spread_out(mean, wcen, 0)
        spread_out(inverse, winv, 0)

        def window_step(i, inside):
            for at in (1, 2):
                @when(taker & (i == 2 * at - 1))
                def _():
                    far_take(at)

            window_row(i, e0, e1, wcen, tc, tr, spec)
            return inside

        lax.fori_loop(0, 4, window_step, 0)

        @when(n == 0)
        def _():
            extended()
            px[1] = wx[WM - PM:WM - PM + PROWS, :]

        @when((n == 1) & odd)
        def _():
            whole.wait_recv()

        @when(taker)
        def _():
            take_cols(0)
            start(pcorners)
            take_cols(1)
            take_cols(2)
            wait_recv(prows)
            wait_recv(pcorners)

        def phase(h, inside):
            @when(taker & (h == 1))
            def _():
                take_cols(3)

            patch_moments(px, 1 - n, 2 * STRIDE * h, pcen, pinv)

            def patch_step(m, deeper):
                @when(taker & (h == 0) & (m == 1))
                def _():
                    far_take(3)

                patch_row(2 * h + m, px, 1 - n, m, pcen, pinv, winv, tc, tr, t4, spec, peak)
                return deeper

            return lax.fori_loop(0, 2, patch_step, inside)

        lax.fori_loop(0, 2, phase, 0)
        finish(peak, res, n)
        return carry

    lax.fori_loop(jnp.where(last, 0, jnp.where(first, 2, 1)), 2, work, 0)

    @when(inner)
    def _():
        back.start()

    wait_send(wcols)
    wait_send(wrows)
    wait_send(wcorners)

    @when(taker)
    def _():
        wait_send(prows)
        wait_send(pcorners)
        for copies in pcols:
            wait_send(copies)

    @when(sender)
    def _():
        for copy in far:
            copy.wait_send()

    @when(even)
    def _():
        whole.wait_send()

    @when(inner)
    def _():
        back.wait_send()

    @when(last)
    def _():
        out_ref[0] = res[0]

    @when(jnp.logical_not(last))
    def _():
        back.wait_recv()
        out_ref[0] = res_in[...]


def place(in_ref, flow_ref, strength_ref):
    flow_ref[0, 0] = in_ref[0, 0:2, 0:COUNT]
    strength_ref[0] = in_ref[0, 2:3, 0:COUNT]


def solution(mesh):
    tabs = tables()

    def local(sections, following):
        dma = pltpu.SemaphoreType.DMA
        vmem = pltpu.VMEM
        found = pl.pallas_call(
            kernel,
            out_shape=jax.ShapeDtypeStruct((1, 8, LANE), F32),
            in_specs=[pl.BlockSpec(memory_space=pl.ANY)] * 5,
            out_specs=pl.BlockSpec(memory_space=vmem),
            scratch_shapes=[
                vmem((WIN, WIN), BF16), vmem((WIN, WIN), BF16), vmem((2 * WIN, WIN), BF16),
                vmem((WROWS, WIDE), F32),
                vmem((2, PROWS, WIDE), F32),
                vmem((WROWS, SPAN), F32),
                vmem((WROWS, SPAN - STRIDE), F32),
                vmem((8, 8, LANE), F32), vmem((8, 8, LANE), F32), vmem((8, 8, LANE), F32), vmem((8, 8, LANE), F32),
                vmem((16, 4, PATCH, WIN), BF16),
                vmem((3, COUNT, 8, LANE), F32),
                vmem((2 * CUTS, 16, LANE), F32),
                vmem((2 * CUTS, 16, LANE), F32),
                vmem((2, 8, LANE), F32),
                vmem((8, LANE), F32),
                dma((5,)), dma((8,)), dma((8,)), dma((CUTS + 2,)), dma((CUTS + 2,)),
                dma((6,)), dma((6,)), dma((2 * CUTS,)), dma((2 * CUTS,)), dma((2,)),
                pltpu.SemaphoreType.REGULAR,
            ],
            compiler_params=pltpu.CompilerParams(collective_id=0, has_side_effects=True, vmem_limit_bytes=58 * 2**20),
            name="patch_flow",
        )(sections, following, *[jnp.asarray(v) for v in tabs])
        return tuple(pl.pallas_call(
            place,
            out_shape=(jax.ShapeDtypeStruct((1, 1, 2, COUNT), F32), jax.ShapeDtypeStruct((1, 1, COUNT), F32)),
            in_specs=[pl.BlockSpec(memory_space=vmem)],
            out_specs=(pl.BlockSpec(memory_space=vmem),) * 2,
            name="place",
        )(found))

    return jax.shard_map(
        local,
        mesh=mesh,
        in_specs=(P("sec", "tile", None, None), P("tile", None, None)),
        out_specs=(P("sec", "tile", None, None), P("sec", "tile", None)),
        check_vma=False,
    )
```

```python
import jax
import jax.numpy as jnp
import ml_dtypes
import numpy as np
from jax import lax
from jax.experimental import pallas as pl
from jax.experimental.pallas import tpu as pltpu
from jax.sharding import PartitionSpec as P

MESH = pl.DeviceIdType.MESH
F32 = jnp.float32
BF16 = jnp.bfloat16

PATCH = 128
WIN = 256
TH = 256
TW = 512
TCOLS = 4
TROWS = 4
SECS = 16
STRIDE = 64
WM = 96
PM = 32
LANE = 128
WROWS = TH + 2 * WM
PROWS = TH + 2 * PM
WIDE = TW + 2 * LANE
SPAN = TW + 2 * WM
COUNT = 32


def tables():
    b = np.arange(WIN)[:, None]
    turn = (b * (2 * np.arange(PATCH)[None, :] + 1)) % (2 * WIN)
    angle = turn * (np.pi / WIN)
    tc = np.concatenate([np.cos(angle), np.sin(angle)], 1)
    cr, sr = tc[:PATCH, :PATCH].T, tc[:PATCH, PATCH:].T
    four = np.concatenate([np.concatenate(x, 1) for x in ((cr, -sr), (sr, cr), (cr, sr), (-sr, cr))], 0)
    return [np.ascontiguousarray(v).astype(np.float32).astype(ml_dtypes.bfloat16) for v in (tc, tc.T, four)]


def dot(a, b):
    return jnp.dot(a, b, preferred_element_type=F32)


def tree(x):
    rows = x.shape[0]
    while rows > 8:
        rows //= 2
        x = x[:rows] + x[rows:]
    for h in (4, 2, 1):
        x = x + pltpu.roll(x, h, 0)
    return x


def fold(x):
    rows = x.shape[0]
    while rows > 8:
        rows //= 2
        x = x[:rows] + x[rows:]
    return sum((x[:, a:a + LANE] for a in range(LANE, x.shape[1], LANE)), x[:, :LANE])


def total(x):
    return jnp.sum(jnp.sum(x, axis=-2, keepdims=True), axis=-1, keepdims=True)


def inner_centres(wx, slot, wcen):
    strips = [tree(wx[slot, STRIDE * i:STRIDE * i + STRIDE, LANE:LANE + TW]) for i in (2, 3, 4)]
    middle = strips[0] + strips[1] + strips[2]
    sub = lax.broadcasted_iota(jnp.int32, middle.shape, 0)
    sums = jnp.where(sub == 0, middle - strips[2], jnp.where(sub == 3, middle - strips[0], middle))
    h = 1
    while h < STRIDE:
        sums = sums + pltpu.roll(sums, TW - h, 1)
        h *= 2
    rows = jnp.where((sub == 0) | (sub == 3), 2.0 * STRIDE, 3.0 * STRIDE)[:, 0:1]
    blocks = [sums[:, PM + STRIDE * m:PM + STRIDE * m + 1] for m in range(7)]
    for j in range(8):
        part = blocks[max(0, j - 2):min(7, j + 2)]
        wcen[j] = jnp.broadcast_to(sum(part[1:], part[0]) / (rows * float(STRIDE * len(part))), (8, LANE))


def window_row(i, wx, slot, cen, sums, tc, tr, spec):
    rows = pl.ds(pl.multiple_of(i * STRIDE, STRIDE), WIN)
    for j in range(8):
        lane = LANE - WM + STRIDE * j
        x = wx[slot, rows, pl.ds(lane // LANE * LANE, WIN + LANE)][:, lane % LANE:lane % LANE + WIN]
        x = x - cen[j, pl.ds(i, 1), 0:1]
        sums[0, i * 8 + j] = fold(x)
        sums[1, i * 8 + j] = fold(x * x)
        z = dot(tr[...], dot(x.astype(BF16), tc[...]).astype(BF16))
        p, r = z[:PATCH, :PATCH], z[:PATCH, PATCH:]
        t, q = z[PATCH:, :PATCH], z[PATCH:, PATCH:]
        for m, g in enumerate((p - q, r + t, p + q, r - t)):
            spec[i * 4 + j // 2, m, :, pl.ds(LANE * (j % 2), LANE)] = g.astype(BF16)


def cross(f, g):
    xr = f[0] * g[0] + f[1] * g[1]
    xi = f[0] * g[1] - f[1] * g[0]
    yr = f[2] * g[2] + f[3] * g[3]
    yi = f[2] * g[3] - f[3] * g[2]
    return [xr + yr, xi + yi, xi - yi, yr - xr]


def window_scales(sums, winv):
    mean = total(sums[0]) * (1.0 / (WIN * WIN))
    spread = total(sums[1]) * (1.0 / (WIN * WIN)) - mean * mean
    winv[...] = jnp.broadcast_to(lax.rsqrt(jnp.maximum(spread, 0.0) + 1e-5), winv.shape)


def patch_row(i, px, slot, winv, tc, tr, t4, spec, peak):
    offset = lax.broadcasted_iota(jnp.int32, (PATCH // 8, 8, PATCH), 0) * 8
    offset = offset + lax.broadcasted_iota(jnp.int32, (PATCH // 8, 8, PATCH), 1)
    offset = (offset - PATCH // 2).astype(F32)
    band = px[slot, pl.ds(pl.multiple_of(STRIDE * i, STRIDE), PATCH), :]
    x = [band[:, LANE - PM + STRIDE * j:LANE - PM + STRIDE * j + PATCH] for j in range(8)]
    centres = [total(fold(v)) * (1.0 / (PATCH * PATCH)) for v in x]
    x = [v - m for v, m in zip(x, centres)]
    scales = []
    for j in range(8):
        spread = total(fold(x[j] * x[j])) * (1.0 / (PATCH * PATCH))
        scales.append(lax.rsqrt(spread + 1e-5) * winv[i * 8 + j] * (1.0 / (32768.0 * 128.0)))
    x = [v.astype(BF16) for v in x]
    a = dot(jnp.concatenate(x, 0), tc[:PATCH, :]).astype(BF16)
    fs = []
    for jj in range(4):
        e, o = a[256 * jj:256 * jj + 128], a[256 * jj + 128:256 * jj + 256]
        upper = jnp.concatenate([e[:, :LANE], o[:, :LANE]], 1)
        lower = jnp.concatenate([e[:, LANE:], o[:, LANE:]], 1)
        fs.append(dot(t4[...], jnp.concatenate([upper, lower], 0)).astype(BF16))
    lhs = []
    for jj in range(4):
        f = [fs[jj][LANE * n:LANE * n + LANE] for n in range(4)]
        ar, ai, di, dr = cross(f, [spec[i * 4 + jj, n] for n in range(4)])
        for k in range(2):
            h = slice(LANE * k, LANE * k + LANE)
            lhs += [jnp.concatenate([ar[:, h], ai[:, h]], 1), jnp.concatenate([di[:, h], dr[:, h]], 1)]
    uv = dot(jnp.concatenate(lhs, 0), tr[:, :PATCH]).astype(BF16)
    for jj in range(4):
        s = dot(tc[:PATCH, :], jnp.concatenate([uv[512 * jj:512 * jj + 256], uv[512 * jj + 256:512 * jj + 512]], 1))
        for k in range(2):
            j = 2 * jj + k
            score = s[:, LANE * k:LANE * k + LANE].reshape(PATCH // 8, 8, PATCH) * scales[j]
            high = jnp.max(score, axis=0)
            weight = jnp.exp(score - high[None])
            peak[0, i * 8 + j] = high
            peak[1, i * 8 + j] = jnp.sum(weight, axis=0)
            peak[2, i * 8 + j] = jnp.sum(weight * offset, axis=0)


def finish(peak, res, slot):
    high = peak[0]
    top = jnp.max(jnp.max(high, axis=1, keepdims=True), axis=2, keepdims=True)
    scale = jnp.exp(high - top)
    weight = peak[1] * scale
    column = (lax.broadcasted_iota(jnp.int32, (COUNT, 8, LANE), 2) - PATCH // 2).astype(F32)

    whole = total(weight)
    by_row = total(peak[2] * scale) / whole
    by_col = total(weight * column) / whole
    strength = (top + jnp.log(whole)) * (1.0 / 128.0)
    place = lax.broadcasted_iota(jnp.int32, (COUNT, 1, LANE), 0) == lax.broadcasted_iota(jnp.int32, (COUNT, 1, LANE), 2)
    for k, v in enumerate((by_row, by_col, strength)):
        res[slot, k:k + 1, :] = jnp.sum(jnp.where(place, v, 0.0), axis=0)


def pack(x, lane):
    group = lax.broadcasted_iota(jnp.int32, (16, LANE), 1) // PM
    out = jnp.zeros((16, LANE), F32)
    for g in range(4):
        part = x[16 * g:16 * g + 16]
        shift = (PM * g - lane) % LANE
        out = jnp.where(group == g, pltpu.roll(part, shift, 1) if shift else part, out)
    return out


def unpack(y, lane):
    out = []
    for g in range(4):
        shift = (lane - PM * g) % LANE
        out.append(pltpu.roll(y, shift, 1) if shift else y)
    return jnp.concatenate(out, 0)


def when(ok):
    return pl.when(ok)


def kernel(sec_ref, fol_ref, tc_ref, tr_ref, t4_ref, out_ref,
           tc, tr, t4, wx, px, e0, wcen, sums, winv, spec, peak, out_cols, in_cols, res, res_in,
           lsem, wsend, wrecv, fsend, frecv, psend, precv, rsem, grant_sem):
    s, t = lax.axis_index("sec"), lax.axis_index("tile")
    r, c = t // TCOLS, lax.rem(t, TCOLS)
    after, before = lax.rem(s + 1, SECS), lax.rem(s + SECS - 1, SECS)
    has_up, has_down, has_left, has_right = r > 0, r < TROWS - 1, c > 0, c < TCOLS - 1
    left, right = (s, t - 1), (s, t + 1)
    first, last = s == 0, s == SECS - 1
    inner = s > 0
    even = lax.rem(s, 2) == 0
    odd = jnp.logical_not(even)
    taker = even & inner
    sender = odd & jnp.logical_not(last)
    eager = lax.rem(s // 2, 2) == 1
    steps = [(has_left, -1), (has_right, 1), (has_up, -TCOLS), (has_down, TCOLS)]
    steps += [(a & b, m + n) for a, m in steps[:2] for b, n in steps[2:]]
    near = sum(ok.astype(jnp.int32) for ok, _ in steps)

    barrier = pltpu.get_barrier_semaphore()

    def signal(sem, d):
        pl.semaphore_signal(sem, inc=1, device_id=d, device_id_type=MESH)

    evens = jnp.where(even, s, before)
    for ok, step in steps:
        @when(ok)
        def _():
            signal(barrier, (evens, t + step))

    @when(inner)
    def _():
        signal(barrier, (before, t))

    own = sec_ref.at[0, 0]
    constants = [pltpu.make_async_copy(a, b, lsem.at[2 + n]) for n, (a, b) in enumerate(((tc_ref, tc), (tr_ref, tr), (t4_ref, t4)))]
    centre = pltpu.make_async_copy(own, wx.at[0, pl.ds(WM, TH), pl.ds(LANE, TW)], lsem.at[0])
    spare = pltpu.make_async_copy(fol_ref.at[0], e0, lsem.at[1])
    centre.start()

    @when(last)
    def _():
        spare.start()

    for copy in constants:
        copy.start()

    @when(jnp.logical_not(has_up))
    def _():
        wx[0, 0:WM, :] = jnp.zeros((WM, WIDE), F32)

        @when(taker)
        def _():
            px[0, 0:PM, LANE:LANE + TW] = jnp.zeros((PM, TW), F32)

    @when(jnp.logical_not(has_down))
    def _():
        wx[0, WM + TH:, :] = jnp.zeros((WM, WIDE), F32)

        @when(taker)
        def _():
            px[0, PM + TH:, LANE:LANE + TW] = jnp.zeros((PM, TW), F32)

    @when(jnp.logical_not(has_left))
    def _():
        wx[0, :, 0:LANE] = jnp.zeros((WROWS, LANE), F32)

    @when(jnp.logical_not(has_right))
    def _():
        wx[0, :, LANE + TW:] = jnp.zeros((WROWS, LANE), F32)

    res[...] = jnp.zeros(res.shape, F32)

    @when(even)
    def _():
        pl.semaphore_wait(barrier, 2 * near + 1)

        @when(jnp.logical_not(eager))
        def _():
            signal(grant_sem, (after, t))

    def remote(src, dst, ssem, rsem, d):
        return pltpu.make_async_remote_copy(src_ref=src, dst_ref=dst, send_sem=ssem, recv_sem=rsem,
                                            device_id=d, device_id_type=MESH)

    def start(copies):
        for ok, _, copy in copies:
            @when(ok)
            def _():
                copy.start()

    def wait_recv(copies):
        for _, ok, copy in copies:
            @when(ok)
            def _():
                copy.wait_recv()

    def wait_send(copies):
        for ok, _, copy in copies:
            @when(ok)
            def _():
                copy.wait_send()

    def ring(src, at, buf, to, m, ssem, rsem, base):
        r0, c0 = at
        out = []
        edge = c0 + TW - LANE
        for k, (vert, opposite, row, dst, step) in enumerate((
                (has_up, has_down, r0, m + TH, -TCOLS), (has_down, has_up, r0 + TH - m, 0, TCOLS))):
            for n, (side, other, lane, width, dlane, move) in enumerate((
                    (None, None, c0, TW, LANE, 0), (has_left, has_right, c0, LANE, LANE + TW, -1), (has_right, has_left, edge, LANE, 0, 1))):
                sends = vert if side is None else vert & side
                takes = opposite if side is None else opposite & other
                out.append((sends, takes, remote(
                    src.at[pl.ds(row, m), pl.ds(lane, width)], buf.at[to, pl.ds(dst, m), pl.ds(dlane, width)],
                    ssem.at[base + 3 * k + n], rsem.at[base + 3 * k + n], (s, t + step + move))))
        return out

    edge = TW - LANE
    wmargins = ring(own, (0, 0), wx, 0, WM, wsend, wrecv, 2)
    wmargins = [
        (has_left, has_right, remote(own.at[:, pl.ds(0, LANE)], wx.at[0, pl.ds(WM, TH), pl.ds(LANE + TW, LANE)], wsend.at[0], wrecv.at[0], left)),
        (has_right, has_left, remote(own.at[:, pl.ds(edge, LANE)], wx.at[0, pl.ds(WM, TH), pl.ds(0, LANE)], wsend.at[1], wrecv.at[1], right)),
    ] + wmargins

    ranges = [(0, PM), (TH - PM, PM)] + [(PM + STRIDE * n, STRIDE) for n in range(3)]
    pieces = [(own.at[pl.ds(a, n)], px.at[0, pl.ds(PM + a, n), pl.ds(LANE, TW)]) for a, n in ranges]
    pieces += [(out_cols.at[pl.ds(a, n)], in_cols.at[pl.ds(a, n)]) for a, n in ((0, 6), (6, 4))]
    far = [remote(a, b, fsend.at[k], frecv.at[k], (after, t)) for k, (a, b) in enumerate(pieces)]
    whole = remote(wx.at[0, pl.ds(WM - PM, PROWS)], px.at[0], fsend.at[7], frecv.at[7], (after, t))

    def far_start(copies):
        @when(sender)
        def _():
            for copy in copies:
                copy.start()

    def far_permission():
        @when(sender)
        def _():
            pl.semaphore_wait(barrier, 1)

    @when(even)
    def _():
        start(wmargins)

    @when(odd & jnp.logical_not(last))
    def _():
        pl.semaphore_wait(grant_sem, 1)
        start(wmargins)
        far_permission()
        far_start(far[:4])

    pmargins = [
        (has_up, has_down, remote(px.at[0, pl.ds(PM, PM), pl.ds(LANE, TW)], px.at[0, pl.ds(PM + TH, PM), pl.ds(LANE, TW)], psend.at[0], precv.at[0], (s, t - TCOLS))),
        (has_down, has_up, remote(px.at[0, pl.ds(TH, PM), pl.ds(LANE, TW)], px.at[0, pl.ds(0, PM), pl.ds(LANE, TW)], psend.at[1], precv.at[1], (s, t + TCOLS))),
    ]

    def send_cols():
        for k in range(5):
            row = WM - PM + STRIDE * k
            out_cols[2 * k] = pack(wx[0, row:row + STRIDE, 0:LANE], LANE - PM)
            out_cols[2 * k + 1] = pack(wx[0, row:row + STRIDE, LANE + TW:], 0)
        far_start([far[5], far[4], far[6]])

    def take_cols(strips):
        for k in strips:
            row = STRIDE * k
            px[0, row:row + STRIDE, 0:LANE] = unpack(in_cols[2 * k], LANE - PM)
            px[0, row:row + STRIDE, LANE + TW:] = unpack(in_cols[2 * k + 1], 0)

    def far_take(numbers):
        for k in numbers:
            far[k].wait_recv()

    for copy in constants:
        copy.wait()
    centre.wait()

    def extended():
        wait_recv(wmargins)

        @when(even)
        def _():
            whole.start()

        @when(even & eager)
        def _():
            signal(grant_sem, (after, t))

    @when(first)
    def _():
        extended()

    back = remote(res.at[1], res_in, rsem.at[0], rsem.at[1], (before, t))

    def work(n, carry):
        slot = 1 - n

        @when(n == 0)
        def _():
            spare.wait()
            wx[1] = jnp.concatenate([jnp.zeros((WROWS, PM), F32), e0[...], jnp.zeros((WROWS, PM), F32)], 1)

        inner_centres(wx, slot, wcen)

        @when((n == 1) & jnp.logical_not(last))
        def _():
            extended()

        @when(sender)
        def _():
            send_cols()

        def window_step(i, inside):
            @when(taker & (i == 2))
            def _():
                far_take((0, 1))
                start(pmargins)

            window_row(i, wx, slot, wcen, sums, tc, tr, spec)
            return inside

        lax.fori_loop(0, 4, window_step, 0)

        @when(n == 0)
        def _():
            pl.semaphore_wait(grant_sem, 1)
            start(wmargins)
            extended()
            px[1] = wx[0, WM - PM:WM - PM + PROWS, :]

        window_scales(sums, winv)

        @when((n == 1) & odd)
        def _():
            whole.wait_recv()

        @when(taker)
        def _():
            far_take((2, 3, 5))
            take_cols((0, 1, 2))
            wait_recv(pmargins)

        def phase(h, inside):
            @when(taker & (h == 1))
            def _():
                far_take((4, 6))
                take_cols((3, 4))

            def patch_step(m, deeper):
                patch_row(2 * h + m, px, 1 - n, winv, tc, tr, t4, spec, peak)
                return deeper

            return lax.fori_loop(0, 2, patch_step, inside)

        lax.fori_loop(0, 2, phase, 0)
        finish(peak, res, n)
        return carry

    lax.fori_loop(jnp.where(last, 0, jnp.where(first, 2, 1)), 2, work, 0)

    @when(inner)
    def _():
        back.start()

    wait_send(wmargins)

    @when(taker)
    def _():
        wait_send(pmargins)

    @when(sender)
    def _():
        for copy in far:
            copy.wait_send()

    @when(even)
    def _():
        whole.wait_send()

    @when(inner)
    def _():
        back.wait_send()

    @when(last)
    def _():
        out_ref[0] = res[0]

    @when(jnp.logical_not(last))
    def _():
        back.wait_recv()
        out_ref[0] = res_in[...]


def place(in_ref, flow_ref, strength_ref):
    flow_ref[0, 0] = in_ref[0, 0:2, 0:COUNT]
    strength_ref[0] = in_ref[0, 2:3, 0:COUNT]


def solution(mesh):
    tabs = tables()

    def local(sections, following):
        dma = pltpu.SemaphoreType.DMA
        vmem = pltpu.VMEM
        found = pl.pallas_call(
            kernel,
            out_shape=jax.ShapeDtypeStruct((1, 8, LANE), F32),
            in_specs=[pl.BlockSpec(memory_space=pl.ANY)] * 5,
            out_specs=pl.BlockSpec(memory_space=vmem),
            scratch_shapes=[
                vmem((WIN, WIN), BF16), vmem((WIN, WIN), BF16), vmem((2 * WIN, WIN), BF16),
                vmem((2, WROWS, WIDE), F32),
                vmem((2, PROWS, WIDE), F32),
                vmem((WROWS, SPAN), F32),
                vmem((8, 8, LANE), F32),
                vmem((2, COUNT, 8, LANE), F32),
                vmem((COUNT, 1, LANE), F32),
                vmem((16, 4, PATCH, WIN), BF16),
                vmem((3, COUNT, 8, LANE), F32),
                vmem((10, 16, LANE), F32),
                vmem((10, 16, LANE), F32),
                vmem((2, 8, LANE), F32),
                vmem((8, LANE), F32),
                dma((5,)), dma((8,)), dma((8,)), dma((8,)), dma((8,)), dma((2,)), dma((2,)), dma((2,)),
                pltpu.SemaphoreType.REGULAR,
            ],
            compiler_params=pltpu.CompilerParams(collective_id=0, has_side_effects=True, vmem_limit_bytes=58 * 2**20),
            name="patch_flow",
        )(sections, following, *[jnp.asarray(v) for v in tabs])
        return tuple(pl.pallas_call(
            place,
            out_shape=(jax.ShapeDtypeStruct((1, 1, 2, COUNT), F32), jax.ShapeDtypeStruct((1, 1, COUNT), F32)),
            in_specs=[pl.BlockSpec(memory_space=vmem)],
            out_specs=(pl.BlockSpec(memory_space=vmem),) * 2,
            name="place",
        )(found))

    return jax.shard_map(
        local,
        mesh=mesh,
        in_specs=(P("sec", "tile", None, None), P("tile", None, None)),
        out_specs=(P("sec", "tile", None, None), P("sec", "tile", None)),
        check_vma=False,
    )
```

```python
import jax
import jax.numpy as jnp
import ml_dtypes
import numpy as np
from jax import lax
from jax.experimental import pallas as pl
from jax.experimental.pallas import tpu as pltpu
from jax.sharding import PartitionSpec as P

MESH = pl.DeviceIdType.MESH
F32 = jnp.float32
BF16 = jnp.bfloat16

PATCH = 128
WIN = 256
TH = 256
TW = 512
TCOLS = 4
TROWS = 4
SECS = 16
STRIDE = 64
WM = 96
PM = 32
LANE = 128
WROWS = TH + 2 * WM
PROWS = TH + 2 * PM
WIDE = TW + 2 * LANE
SPAN = TW + 2 * WM
COUNT = 32


def tables():
    b = np.arange(WIN)[:, None]
    turn = (b * (2 * np.arange(PATCH)[None, :] + 1)) % (2 * WIN)
    angle = turn * (np.pi / WIN)
    tc = np.concatenate([np.cos(angle), np.sin(angle)], 1)
    cr, sr = tc[:PATCH, :PATCH].T, tc[:PATCH, PATCH:].T
    four = np.concatenate([np.concatenate(x, 1) for x in ((cr, -sr), (sr, cr), (cr, sr), (-sr, cr))], 0)
    return [np.ascontiguousarray(v).astype(np.float32).astype(ml_dtypes.bfloat16) for v in (tc, tc.T, four)]


def dot(a, b):
    return jnp.dot(a, b, preferred_element_type=F32)


def tree(x):
    rows = x.shape[0]
    while rows > 8:
        rows //= 2
        x = x[:rows] + x[rows:]
    for h in (4, 2, 1):
        x = x + pltpu.roll(x, h, 0)
    return x


def fold(x):
    rows = x.shape[0]
    while rows > 8:
        rows //= 2
        x = x[:rows] + x[rows:]
    return sum((x[:, a:a + LANE] for a in range(LANE, x.shape[1], LANE)), x[:, :LANE])


def total(x):
    return jnp.sum(jnp.sum(x, axis=-2, keepdims=True), axis=-1, keepdims=True)


def inner_centres(wx, slot, wcen):
    strips = [tree(wx[slot, STRIDE * i:STRIDE * i + STRIDE, LANE:LANE + TW]) for i in (2, 3, 4)]
    middle = strips[0] + strips[1] + strips[2]
    sub = lax.broadcasted_iota(jnp.int32, middle.shape, 0)
    sums = jnp.where(sub == 0, middle - strips[2], jnp.where(sub == 3, middle - strips[0], middle))
    h = 1
    while h < STRIDE:
        sums = sums + pltpu.roll(sums, TW - h, 1)
        h *= 2
    rows = jnp.where((sub == 0) | (sub == 3), 2.0 * STRIDE, 3.0 * STRIDE)[:, 0:1]
    blocks = [sums[:, PM + STRIDE * m:PM + STRIDE * m + 1] for m in range(7)]
    for j in range(8):
        part = blocks[max(0, j - 2):min(7, j + 2)]
        wcen[j] = jnp.broadcast_to(sum(part[1:], part[0]) / (rows * float(STRIDE * len(part))), (8, LANE))


def window_row(i, wx, slot, cen, sums, tc, tr, spec):
    rows = pl.ds(pl.multiple_of(i * STRIDE, STRIDE), WIN)
    for j in range(8):
        lane = LANE - WM + STRIDE * j
        x = wx[slot, rows, pl.ds(lane // LANE * LANE, WIN + LANE)][:, lane % LANE:lane % LANE + WIN]
        x = x - cen[j, pl.ds(i, 1), 0:1]
        sums[0, i * 8 + j] = fold(x)
        sums[1, i * 8 + j] = fold(x * x)
        z = dot(tr[...], dot(x.astype(BF16), tc[...]).astype(BF16))
        p, r = z[:PATCH, :PATCH], z[:PATCH, PATCH:]
        t, q = z[PATCH:, :PATCH], z[PATCH:, PATCH:]
        for m, g in enumerate((p - q, r + t, p + q, r - t)):
            spec[i * 4 + j // 2, m, :, pl.ds(LANE * (j % 2), LANE)] = g.astype(BF16)


def cross(f, g):
    xr = f[0] * g[0] + f[1] * g[1]
    xi = f[0] * g[1] - f[1] * g[0]
    yr = f[2] * g[2] + f[3] * g[3]
    yi = f[2] * g[3] - f[3] * g[2]
    return [xr + yr, xi + yi, xi - yi, yr - xr]


def window_scales(sums, winv):
    mean = total(sums[0]) * (1.0 / (WIN * WIN))
    spread = total(sums[1]) * (1.0 / (WIN * WIN)) - mean * mean
    winv[...] = jnp.broadcast_to(lax.rsqrt(jnp.maximum(spread, 0.0) + 1e-5), winv.shape)


def patch_row(i, px, slot, winv, tc, tr, t4, spec, peak):
    offset = lax.broadcasted_iota(jnp.int32, (PATCH // 8, 8, PATCH), 0) * 8
    offset = offset + lax.broadcasted_iota(jnp.int32, (PATCH // 8, 8, PATCH), 1)
    offset = (offset - PATCH // 2).astype(F32)
    band = px[slot, pl.ds(pl.multiple_of(STRIDE * i, STRIDE), PATCH), :]
    x = [band[:, LANE - PM + STRIDE * j:LANE - PM + STRIDE * j + PATCH] for j in range(8)]
    centres = [total(fold(v)) * (1.0 / (PATCH * PATCH)) for v in x]
    x = [v - m for v, m in zip(x, centres)]
    scales = []
    for j in range(8):
        spread = total(fold(x[j] * x[j])) * (1.0 / (PATCH * PATCH))
        scales.append(lax.rsqrt(spread + 1e-5) * winv[i * 8 + j] * (1.0 / (32768.0 * 128.0)))
    x = [v.astype(BF16) for v in x]
    a = dot(jnp.concatenate(x, 0), tc[:PATCH, :]).astype(BF16)
    fs = []
    for jj in range(4):
        e, o = a[256 * jj:256 * jj + 128], a[256 * jj + 128:256 * jj + 256]
        upper = jnp.concatenate([e[:, :LANE], o[:, :LANE]], 1)
        lower = jnp.concatenate([e[:, LANE:], o[:, LANE:]], 1)
        fs.append(dot(t4[...], jnp.concatenate([upper, lower], 0)).astype(BF16))
    lhs = []
    for jj in range(4):
        f = [fs[jj][LANE * n:LANE * n + LANE] for n in range(4)]
        ar, ai, di, dr = cross(f, [spec[i * 4 + jj, n] for n in range(4)])
        for k in range(2):
            h = slice(LANE * k, LANE * k + LANE)
            lhs += [jnp.concatenate([ar[:, h], ai[:, h]], 1), jnp.concatenate([di[:, h], dr[:, h]], 1)]
    uv = dot(jnp.concatenate(lhs, 0), tr[:, :PATCH]).astype(BF16)
    for jj in range(4):
        s = dot(tc[:PATCH, :], jnp.concatenate([uv[512 * jj:512 * jj + 256], uv[512 * jj + 256:512 * jj + 512]], 1))
        for k in range(2):
            j = 2 * jj + k
            score = s[:, LANE * k:LANE * k + LANE].reshape(PATCH // 8, 8, PATCH) * scales[j]
            high = jnp.max(score, axis=0)
            weight = jnp.exp(score - high[None])
            peak[0, i * 8 + j] = high
            peak[1, i * 8 + j] = jnp.sum(weight, axis=0)
            peak[2, i * 8 + j] = jnp.sum(weight * offset, axis=0)


def finish(peak, res, slot):
    high = peak[0]
    top = jnp.max(jnp.max(high, axis=1, keepdims=True), axis=2, keepdims=True)
    scale = jnp.exp(high - top)
    weight = peak[1] * scale
    column = (lax.broadcasted_iota(jnp.int32, (COUNT, 8, LANE), 2) - PATCH // 2).astype(F32)

    whole = total(weight)
    by_row = total(peak[2] * scale) / whole
    by_col = total(weight * column) / whole
    strength = (top + jnp.log(whole)) * (1.0 / 128.0)
    place = lax.broadcasted_iota(jnp.int32, (COUNT, 1, LANE), 0) == lax.broadcasted_iota(jnp.int32, (COUNT, 1, LANE), 2)
    for k, v in enumerate((by_row, by_col, strength)):
        res[slot, k:k + 1, :] = jnp.sum(jnp.where(place, v, 0.0), axis=0)


def pack(x, lane):
    group = lax.broadcasted_iota(jnp.int32, (16, LANE), 1) // PM
    out = jnp.zeros((16, LANE), F32)
    for g in range(4):
        part = x[16 * g:16 * g + 16]
        shift = (PM * g - lane) % LANE
        out = jnp.where(group == g, pltpu.roll(part, shift, 1) if shift else part, out)
    return out


def unpack(y, lane):
    out = []
    for g in range(4):
        shift = (lane - PM * g) % LANE
        out.append(pltpu.roll(y, shift, 1) if shift else y)
    return jnp.concatenate(out, 0)


def when(ok):
    return pl.when(ok)


def kernel(sec_ref, fol_ref, tc_ref, tr_ref, t4_ref, out_ref,
           tc, tr, t4, wx, px, e0, wcen, sums, winv, spec, peak, out_cols, in_cols, res, res_in,
           lsem, wsend, wrecv, fsend, frecv, psend, precv, rsem, grant_sem):
    s, t = lax.axis_index("sec"), lax.axis_index("tile")
    r, c = t // TCOLS, lax.rem(t, TCOLS)
    after, before = lax.rem(s + 1, SECS), lax.rem(s + SECS - 1, SECS)
    has_up, has_down, has_left, has_right = r > 0, r < TROWS - 1, c > 0, c < TCOLS - 1
    left, right = (s, t - 1), (s, t + 1)
    first, last = s == 0, s == SECS - 1
    inner = s > 0
    even = lax.rem(s, 2) == 0
    odd = jnp.logical_not(even)
    taker = even & inner
    sender = odd & jnp.logical_not(last)
    eager = lax.rem(s // 2, 2) == 1
    steps = [(has_left, -1), (has_right, 1), (has_up, -TCOLS), (has_down, TCOLS)]
    steps += [(a & b, m + n) for a, m in steps[:2] for b, n in steps[2:]]
    near = sum(ok.astype(jnp.int32) for ok, _ in steps)

    barrier = pltpu.get_barrier_semaphore()

    def signal(sem, d):
        pl.semaphore_signal(sem, inc=1, device_id=d, device_id_type=MESH)

    evens = jnp.where(even, s, before)
    for ok, step in steps:
        @when(ok)
        def _():
            signal(barrier, (evens, t + step))

    @when(inner)
    def _():
        signal(barrier, (before, t))

    own = sec_ref.at[0, 0]
    constants = [pltpu.make_async_copy(a, b, lsem.at[2 + n]) for n, (a, b) in enumerate(((tc_ref, tc), (tr_ref, tr), (t4_ref, t4)))]
    centre = pltpu.make_async_copy(own, wx.at[0, pl.ds(WM, TH), pl.ds(LANE, TW)], lsem.at[0])
    spare = pltpu.make_async_copy(fol_ref.at[0], e0, lsem.at[1])
    centre.start()

    @when(last)
    def _():
        spare.start()

    for copy in constants:
        copy.start()

    @when(jnp.logical_not(has_up))
    def _():
        wx[0, 0:WM, :] = jnp.zeros((WM, WIDE), F32)

        @when(taker)
        def _():
            px[0, 0:PM, LANE:LANE + TW] = jnp.zeros((PM, TW), F32)

    @when(jnp.logical_not(has_down))
    def _():
        wx[0, WM + TH:, :] = jnp.zeros((WM, WIDE), F32)

        @when(taker)
        def _():
            px[0, PM + TH:, LANE:LANE + TW] = jnp.zeros((PM, TW), F32)

    @when(jnp.logical_not(has_left))
    def _():
        wx[0, :, 0:LANE] = jnp.zeros((WROWS, LANE), F32)

    @when(jnp.logical_not(has_right))
    def _():
        wx[0, :, LANE + TW:] = jnp.zeros((WROWS, LANE), F32)

    res[...] = jnp.zeros(res.shape, F32)

    @when(even)
    def _():
        pl.semaphore_wait(barrier, 2 * near + 1)

        signal(grant_sem, (after, t))

    def remote(src, dst, ssem, rsem, d):
        return pltpu.make_async_remote_copy(src_ref=src, dst_ref=dst, send_sem=ssem, recv_sem=rsem,
                                            device_id=d, device_id_type=MESH)

    def start(copies):
        for ok, _, copy in copies:
            @when(ok)
            def _():
                copy.start()

    def wait_recv(copies):
        for _, ok, copy in copies:
            @when(ok)
            def _():
                copy.wait_recv()

    def wait_send(copies):
        for ok, _, copy in copies:
            @when(ok)
            def _():
                copy.wait_send()

    def ring(src, at, buf, to, m, ssem, rsem, base):
        r0, c0 = at
        out = []
        edge = c0 + TW - LANE
        for k, (vert, opposite, row, dst, step) in enumerate((
                (has_up, has_down, r0, m + TH, -TCOLS), (has_down, has_up, r0 + TH - m, 0, TCOLS))):
            for n, (side, other, lane, width, dlane, move) in enumerate((
                    (None, None, c0, TW, LANE, 0), (has_left, has_right, c0, LANE, LANE + TW, -1), (has_right, has_left, edge, LANE, 0, 1))):
                sends = vert if side is None else vert & side
                takes = opposite if side is None else opposite & other
                out.append((sends, takes, remote(
                    src.at[pl.ds(row, m), pl.ds(lane, width)], buf.at[to, pl.ds(dst, m), pl.ds(dlane, width)],
                    ssem.at[base + 3 * k + n], rsem.at[base + 3 * k + n], (s, t + step + move))))
        return out

    edge = TW - LANE
    wmargins = ring(own, (0, 0), wx, 0, WM, wsend, wrecv, 2)
    wmargins = [
        (has_left, has_right, remote(own.at[:, pl.ds(0, LANE)], wx.at[0, pl.ds(WM, TH), pl.ds(LANE + TW, LANE)], wsend.at[0], wrecv.at[0], left)),
        (has_right, has_left, remote(own.at[:, pl.ds(edge, LANE)], wx.at[0, pl.ds(WM, TH), pl.ds(0, LANE)], wsend.at[1], wrecv.at[1], right)),
    ] + wmargins

    ranges = [(0, PM), (TH - PM, PM)] + [(PM + STRIDE * n, STRIDE) for n in range(3)]
    pieces = [(own.at[pl.ds(a, n)], px.at[0, pl.ds(PM + a, n), pl.ds(LANE, TW)]) for a, n in ranges]
    pieces += [(out_cols.at[pl.ds(a, n)], in_cols.at[pl.ds(a, n)]) for a, n in ((0, 6), (6, 4))]
    far = [remote(a, b, fsend.at[k], frecv.at[k], (after, t)) for k, (a, b) in enumerate(pieces)]
    whole = remote(wx.at[0, pl.ds(WM - PM, PROWS)], px.at[0], fsend.at[7], frecv.at[7], (after, t))

    def far_start(copies):
        @when(sender)
        def _():
            for copy in copies:
                copy.start()

    def far_permission():
        @when(sender)
        def _():
            pl.semaphore_wait(barrier, 1)

    @when(even)
    def _():
        start(wmargins)

    @when(odd & jnp.logical_not(last))
    def _():
        pl.semaphore_wait(grant_sem, 1)
        start(wmargins)
        far_permission()
        far_start(far[:4])

    pmargins = [
        (has_up, has_down, remote(px.at[0, pl.ds(PM, PM), pl.ds(LANE, TW)], px.at[0, pl.ds(PM + TH, PM), pl.ds(LANE, TW)], psend.at[0], precv.at[0], (s, t - TCOLS))),
        (has_down, has_up, remote(px.at[0, pl.ds(TH, PM), pl.ds(LANE, TW)], px.at[0, pl.ds(0, PM), pl.ds(LANE, TW)], psend.at[1], precv.at[1], (s, t + TCOLS))),
    ]

    def send_cols():
        for k in range(5):
            row = WM - PM + STRIDE * k
            out_cols[2 * k] = pack(wx[0, row:row + STRIDE, 0:LANE], LANE - PM)
            out_cols[2 * k + 1] = pack(wx[0, row:row + STRIDE, LANE + TW:], 0)
        far_start([far[5], far[4], far[6]])

    def take_cols(strips):
        for k in strips:
            row = STRIDE * k
            px[0, row:row + STRIDE, 0:LANE] = unpack(in_cols[2 * k], LANE - PM)
            px[0, row:row + STRIDE, LANE + TW:] = unpack(in_cols[2 * k + 1], 0)

    def far_take(numbers):
        for k in numbers:
            far[k].wait_recv()

    for copy in constants:
        copy.wait()
    centre.wait()

    def extended():
        wait_recv(wmargins)

        @when(even)
        def _():
            whole.start()

    @when(first)
    def _():
        extended()

    back = remote(res.at[1], res_in, rsem.at[0], rsem.at[1], (before, t))

    def work(n, carry):
        slot = 1 - n

        @when(n == 0)
        def _():
            spare.wait()
            wx[1] = jnp.concatenate([jnp.zeros((WROWS, PM), F32), e0[...], jnp.zeros((WROWS, PM), F32)], 1)

        inner_centres(wx, slot, wcen)

        @when((n == 1) & jnp.logical_not(last))
        def _():
            extended()

        @when(sender)
        def _():
            send_cols()

        def window_step(i, inside):
            @when(taker & (i == 2))
            def _():
                far_take((0, 1))
                start(pmargins)

            window_row(i, wx, slot, wcen, sums, tc, tr, spec)
            return inside

        lax.fori_loop(0, 4, window_step, 0)

        @when(n == 0)
        def _():
            pl.semaphore_wait(grant_sem, 1)
            start(wmargins)
            extended()
            px[1] = wx[0, WM - PM:WM - PM + PROWS, :]

        window_scales(sums, winv)

        @when((n == 1) & odd)
        def _():
            whole.wait_recv()

        @when(taker)
        def _():
            far_take((2, 3, 5))
            take_cols((0, 1, 2))
            wait_recv(pmargins)

        def phase(h, inside):
            @when(taker & (h == 1))
            def _():
                far_take((4, 6))
                take_cols((3, 4))

            def patch_step(m, deeper):
                patch_row(2 * h + m, px, 1 - n, winv, tc, tr, t4, spec, peak)
                return deeper

            return lax.fori_loop(0, 2, patch_step, inside)

        lax.fori_loop(0, 2, phase, 0)
        finish(peak, res, n)
        return carry

    lax.fori_loop(jnp.where(last, 0, jnp.where(first, 2, 1)), 2, work, 0)

    @when(inner)
    def _():
        back.start()

    wait_send(wmargins)

    @when(taker)
    def _():
        wait_send(pmargins)

    @when(sender)
    def _():
        for copy in far:
            copy.wait_send()

    @when(even)
    def _():
        whole.wait_send()

    @when(inner)
    def _():
        back.wait_send()

    @when(last)
    def _():
        out_ref[0] = res[0]

    @when(jnp.logical_not(last))
    def _():
        back.wait_recv()
        out_ref[0] = res_in[...]


def place(in_ref, flow_ref, strength_ref):
    flow_ref[0, 0] = in_ref[0, 0:2, 0:COUNT]
    strength_ref[0] = in_ref[0, 2:3, 0:COUNT]


def solution(mesh):
    tabs = tables()

    def local(sections, following):
        dma = pltpu.SemaphoreType.DMA
        vmem = pltpu.VMEM
        found = pl.pallas_call(
            kernel,
            out_shape=jax.ShapeDtypeStruct((1, 8, LANE), F32),
            in_specs=[pl.BlockSpec(memory_space=pl.ANY)] * 5,
            out_specs=pl.BlockSpec(memory_space=vmem),
            scratch_shapes=[
                vmem((WIN, WIN), BF16), vmem((WIN, WIN), BF16), vmem((2 * WIN, WIN), BF16),
                vmem((2, WROWS, WIDE), F32),
                vmem((2, PROWS, WIDE), F32),
                vmem((WROWS, SPAN), F32),
                vmem((8, 8, LANE), F32),
                vmem((2, COUNT, 8, LANE), F32),
                vmem((COUNT, 1, LANE), F32),
                vmem((16, 4, PATCH, WIN), BF16),
                vmem((3, COUNT, 8, LANE), F32),
                vmem((10, 16, LANE), F32),
                vmem((10, 16, LANE), F32),
                vmem((2, 8, LANE), F32),
                vmem((8, LANE), F32),
                dma((5,)), dma((8,)), dma((8,)), dma((8,)), dma((8,)), dma((2,)), dma((2,)), dma((2,)),
                pltpu.SemaphoreType.REGULAR,
            ],
            compiler_params=pltpu.CompilerParams(collective_id=0, has_side_effects=True, vmem_limit_bytes=58 * 2**20),
            name="patch_flow",
        )(sections, following, *[jnp.asarray(v) for v in tabs])
        return tuple(pl.pallas_call(
            place,
            out_shape=(jax.ShapeDtypeStruct((1, 1, 2, COUNT), F32), jax.ShapeDtypeStruct((1, 1, COUNT), F32)),
            in_specs=[pl.BlockSpec(memory_space=vmem)],
            out_specs=(pl.BlockSpec(memory_space=vmem),) * 2,
            name="place",
        )(found))

    return jax.shard_map(
        local,
        mesh=mesh,
        in_specs=(P("sec", "tile", None, None), P("tile", None, None)),
        out_specs=(P("sec", "tile", None, None), P("sec", "tile", None)),
        check_vma=False,
    )
```
